128 devices in a mesh: lat: 4 (over x_hi, core), lon: 32 (over y, z, x_lo).
Axes of the slice: x: 4 (x_hi: 2, x_lo: 2; x = x_hi * 2 + x_lo), y: 4, z: 4, core: 2. Of those that a mesh axis runs over, the one named last changes fastest.
Arguments:
- tokens: bfloat16 [2, 768, 384, 512], P(None, 'lat', 'lon'), may hold values from -6 to 6
- region: int32 [2, 768, 384], P(None, 'lat', 'lon'), may hold values from 0 to 2
- w_qkv: bfloat16 [512, 1536], replicated, may hold values from -15 to 15
- w_out: bfloat16 [512, 512], replicated, may hold values from -0.25 to 0.25
- w_merge: bfloat16 [2048, 1024], replicated, may hold values from -0.125 to 0.125
Outputs:
- merged: bfloat16 [2, 384, 192, 1024], P(None, ('lat', 'lon'))
The draws below stay inside these ranges and needn't reach their ends.
All inputs are finite; a program needn't handle non-finite values.
Results may differ from the reference program's by a relative error of at most 0.015.
Values may be sent and summed in bfloat16 or wider, within the bound.
A program may use at most 384 MiB of HBM per device.

```python
import math
import jax
import jax.numpy as jnp
from jax import lax

C = 512
HEADS = 16
WIN_LAT = 6
WIN_LON = 12
LEV = 2
ROWS = 768
COLS = 384


def draw_w_qkv(key, part):
    key = jax.random.fold_in(key, 11)
    base = jax.random.truncated_normal(key, -6.0, 6.0, (C, 3 * C), jnp.float32) / math.sqrt(C)
    return base.astype(jnp.bfloat16)


def plant(result, key, low, top_value):
    index_at = [jax.random.randint(jax.random.fold_in(key, axis), (), 0, length) for axis, length in enumerate(result.shape)]
    longest = result.shape.index(max(result.shape))
    neighbour = index_at[:longest] + [(index_at[longest] + 1) % result.shape[longest]] + index_at[longest + 1:]
    return result.at[tuple(index_at)].set(low).at[tuple(neighbour)].set(top_value)


def shard_levels(own_key, dims, split, low, top_value):
    gain, own = 1.0, jax.random.fold_in(own_key, 6)
    for position, shards_of in split:
        draws = jnp.exp(jax.random.uniform(jax.random.fold_in(own, position), (shards_of,), jnp.float32, low / len(split), top_value / len(split)))
        gain = gain * jnp.repeat(draws, dims[position] // shards_of).reshape([-1 if axis == position else 1 for axis in range(len(dims))])
    return gain


def bell_draw(stream_key, extent, deviation, limit, cuts=(), kind=jnp.bfloat16):
    gain = shard_levels(stream_key, extent, cuts, -0.22, 0.18) if cuts else 1.0
    values = jax.random.normal(stream_key, extent, jnp.float32) * deviation * gain
    return jnp.minimum(jnp.maximum(values, -limit), limit).astype(kind)


def setup_inputs(seed: int = 0) -> dict:
    arg_keys = jax.random.split(jax.random.key(seed), 6)
    return {
        "tokens": bell_draw(arg_keys[0], (LEV, ROWS, COLS, C), 1.0, 6.0, ((1, 4), (2, 32))),
        "region": plant(jax.random.randint(arg_keys[1], (LEV, ROWS, COLS), 0, 3), jax.random.fold_in(arg_keys[1], 1), 0, 2).astype(jnp.int32),
        "w_qkv": draw_w_qkv(jax.random.fold_in(arg_keys[5], 71), 0),
        "w_out": bell_draw(arg_keys[3], (C, C), C ** -0.5, 0.25),
        "w_merge": bell_draw(arg_keys[4], (4 * C, 2 * C), (4 * C) ** -0.5, 0.125),
    }


def normalize(values):
    center = values - lax.optimization_barrier(jnp.mean(values, -1, keepdims=True))
    spread = lax.optimization_barrier(jnp.mean(center * center, -1, keepdims=True))
    return center * lax.rsqrt(spread + 1e-05)

def attend_tile(tile, labels, w_qkv):
    level_count, row_count, column_count, channels = tile.shape
    head_size = channels // HEADS
    normed = normalize(tile.astype(jnp.float32)).astype(jnp.bfloat16)
    packed = jnp.dot(normed.reshape(-1, channels), w_qkv, preferred_element_type=jnp.float32).astype(jnp.bfloat16)
    row_windows = row_count // WIN_LAT
    col_windows = column_count // WIN_LON
    window_count = row_windows * col_windows
    window_span = level_count * WIN_LAT * WIN_LON
    packed = packed.reshape(level_count, row_windows, WIN_LAT, col_windows, WIN_LON, 3, HEADS, head_size)
    packed = packed.transpose(5, 6, 1, 3, 0, 2, 4, 7).reshape(3, HEADS, window_count, window_span, head_size)
    window_labels = labels.reshape(level_count, row_windows, WIN_LAT, col_windows, WIN_LON)
    window_labels = window_labels.transpose(1, 3, 0, 2, 4).reshape(window_count, window_span)
    allowed = window_labels[:, :, None] == window_labels[:, None, :]
    score_scale = head_size ** (-0.5)

    def one_head(head_parts):
        queries, keys_in, values_in = head_parts
        scores = jnp.einsum('wqd,wkd->wqk', queries.astype(jnp.float32), keys_in.astype(jnp.float32)) * score_scale
        scores = jnp.where(allowed, scores, -1e+30)
        peak_score = lax.optimization_barrier(jnp.max(scores, -1, keepdims=True))
        weights = jnp.exp(scores - peak_score)
        weights = (weights / lax.optimization_barrier(jnp.sum(weights, -1, keepdims=True))).astype(jnp.bfloat16)
        return jnp.einsum('wqk,wkd->wqd', weights.astype(jnp.float32), values_in.astype(jnp.float32)).astype(jnp.bfloat16)
    mixed_out = lax.map(one_head, (packed[0], packed[1], packed[2]))
    mixed_out = mixed_out.reshape(HEADS, row_windows, col_windows, level_count, WIN_LAT, WIN_LON, head_size)
    return mixed_out.transpose(3, 1, 4, 2, 5, 0, 6).reshape(level_count, row_count, column_count, channels)

def merge_patches(updated, w_merge):
    level_count, row_count, column_count, channels = updated.shape
    grouped = updated.reshape(level_count, row_count // 2, 2, column_count // 2, 2, channels)
    grouped = grouped.transpose(0, 1, 3, 2, 4, 5).reshape(level_count, row_count // 2, column_count // 2, 4 * channels)
    merge_in = normalize(grouped.astype(jnp.float32)).astype(jnp.bfloat16)
    merged = jnp.dot(merge_in.reshape(-1, 4 * channels), w_merge, preferred_element_type=jnp.float32)
    return merged.astype(jnp.bfloat16).reshape(level_count, row_count // 2, column_count // 2, 2 * channels)

def reference(tokens, region, w_qkv, w_out, w_merge):
    level_count, row_count, column_count, channels = tokens.shape
    half_lat = WIN_LAT // 2
    half_lon = WIN_LON // 2
    rolled = jnp.roll(tokens, (-half_lat, -half_lon), axis=(1, 2))
    initial_row = (jnp.arange(row_count, dtype=jnp.int32) + half_lat) % row_count
    pole_side = (initial_row < half_lat).astype(jnp.int32)
    labels = jnp.roll(region, (-half_lat, -half_lon), axis=(1, 2)) * 2 + pole_side[None, :, None]
    band_count = row_count // WIN_LAT
    tiles = rolled.reshape(level_count, band_count, WIN_LAT, column_count, channels).transpose(1, 0, 2, 3, 4)
    label_tiles = labels.reshape(level_count, band_count, WIN_LAT, column_count).transpose(1, 0, 2, 3)
    mixed_out = lax.map(lambda band_pair: attend_tile(band_pair[0], band_pair[1], w_qkv), (tiles, label_tiles))
    mixed_out = mixed_out.transpose(1, 0, 2, 3, 4).reshape(level_count, row_count, column_count, channels)
    mixed_out = jnp.roll(mixed_out, (half_lat, half_lon), axis=(1, 2))
    attended = jnp.dot(mixed_out.reshape(-1, channels), w_out, preferred_element_type=jnp.float32)
    updated = (tokens.astype(jnp.float32) + attended.reshape(tokens.shape)).astype(jnp.bfloat16)
    return merge_patches(updated, w_merge)
```

```python
import functools

import jax
import jax.numpy as jnp
import numpy as np
from jax import lax
from jax.experimental import pallas as pl
from jax.experimental.pallas import tpu as pltpu
from jax.sharding import PartitionSpec as P

MESH = pl.DeviceIdType.MESH
HEADS = 16
WIN_LAT = 6
WIN_LON = 12
LEV = 2
HALF = 72
SPAN = 144
PADDED = 160
GROUP = 4
F32 = jnp.float32
BF16 = jnp.bfloat16


def tables():
    pick_own = np.zeros((HALF, 192), np.float32)
    pick_west = np.zeros((HALF, 192), np.float32)
    order = np.zeros((PADDED, SPAN), np.float32)
    pack = np.zeros((SPAN, PADDED), np.float32)
    for lev in range(LEV):
        for row in range(6):
            for col in range(6):
                place = (lev * 6 + row) * 6 + col
                pick_own[place, (lev * 6 + row) * 16 + col + 6] = 1
                pick_west[place, (lev * 6 + row) * 16 + col] = 1
    window_rows = ((5, 1, 3), (0, 2, 4))
    for odd in range(2):
        for right in range(2):
            block = odd * 2 + right
            for slot in range(3):
                for lev in range(LEV):
                    for patch in range(6):
                        half, col = divmod(patch, 3)
                        token = half * HALF + (lev * 6 + window_rows[odd][slot]) * 6 + 2 * col + right
                        order[block * 40 + slot * 12 + lev * 6 + patch, token] = 1
    for slot in range(3):
        for lanes in range(4):
            for place in range(12):
                pack[slot * 48 + lanes * 12 + place, lanes * 40 + slot * 12 + place] = 1
    return [jnp.asarray(t, BF16) for t in (pick_own, pick_west, order, pack)]


def dot(a, b):
    return jnp.dot(a, b, preferred_element_type=F32)


def dot_nt(a, b):
    return lax.dot_general(a, b, (((1,), (1,)), ((), ())), preferred_element_type=F32)


def normalize(values):
    center = values - jnp.mean(values, -1, keepdims=True)
    spread = jnp.mean(center * center, -1, keepdims=True)
    return center * lax.rsqrt(spread + 1e-05)


def raw_window(tok, window):
    raw = tok[:, pl.ds(6 * window + 3, 6)]
    return jnp.pad(raw, ((0, 0), (0, 0), (0, 4), (0, 0))).reshape(192, raw.shape[-1])


def fused(
    n_lat,
    n_lon,
    tokens,
    labels,
    pick_own,
    pick_west,
    order,
    pack,
    w_qk_hbm,
    w_vt_hbm,
    w_out_hbm,
    w_merge_hbm,
    recv,
    tok,
    halo,
    west,
    stage,
    w_qk,
    w_vt,
    w_out,
    w_merge,
    xs,
    ns,
    qs,
    ks,
    wos,
    carry,
    odd_save,
    carry_send,
    carry_recv,
    load_sems,
    row_sems,
    halo_send,
    halo_recv,
    carry_sems,
    out_send,
    out_recv,
):
    lat = lax.axis_index("lat")
    lon = lax.axis_index("lon")
    next_lat = lax.rem(lat + 1, n_lat)
    prev_lat = lax.rem(lat + n_lat - 1, n_lat)
    west_lon = lax.rem(lon + n_lon - 1, n_lon)
    rows = tokens.shape[1]
    windows = rows // WIN_LAT
    chunks = windows // GROUP
    span_rows = GROUP * HALF
    first = lax.rem((lon * chunks) // n_lon, chunks)
    first_west = lax.rem((west_lon * chunks) // n_lon, chunks)

    loads = [
        pltpu.make_async_copy(tokens, tok.at[:, pl.ds(0, rows)], load_sems.at[0]),
        pltpu.make_async_copy(w_qk_hbm, w_qk, load_sems.at[1]),
        pltpu.make_async_copy(w_vt_hbm, w_vt, load_sems.at[2]),
        pltpu.make_async_copy(w_out_hbm, w_out, load_sems.at[3]),
        pltpu.make_async_copy(w_merge_hbm, w_merge, load_sems.at[4]),
    ]
    for load in loads:
        load.start()

    barrier = pltpu.get_barrier_semaphore()

    def greet(step, _):
        other = lax.rem(lon + step, n_lon)
        pl.semaphore_signal(barrier, inc=1, device_id=(lat, other), device_id_type=MESH)
        return 0

    lax.fori_loop(1, n_lon, greet, 0)
    pl.semaphore_signal(barrier, inc=1, device_id=(prev_lat, lon), device_id_type=MESH)
    pl.semaphore_signal(barrier, inc=1, device_id=(next_lat, lon), device_id_type=MESH)

    @pl.when(lon == 0)
    def _():
        def greet_before(other, _):
            pl.semaphore_signal(barrier, inc=1, device_id=(prev_lat, other), device_id_type=MESH)
            return 0

        lax.fori_loop(0, n_lon, greet_before, 0)

    loads[0].wait()
    pl.semaphore_wait(barrier, n_lon + 2)

    rows_copy = pltpu.make_async_remote_copy(
        src_ref=tok.at[:, pl.ds(0, 3)],
        dst_ref=tok.at[:, pl.ds(rows, 3)],
        send_sem=row_sems.at[0],
        recv_sem=row_sems.at[1],
        device_id=(prev_lat, lon),
        device_id_type=MESH,
    )
    rows_copy.start()

    def halo_copy(chunk):
        return pltpu.make_async_remote_copy(
            src_ref=west.at[chunk],
            dst_ref=halo.at[chunk],
            send_sem=halo_send.at[chunk],
            recv_sem=halo_recv.at[chunk],
            device_id=(lat, west_lon),
            device_id_type=MESH,
        )

    def send_west(step, _):
        chunk = lax.rem(first_west + step, chunks)

        @pl.when(chunk == chunks - 1)
        def _():
            rows_copy.wait_recv()

        parts = [
            dot(pick_west[...], raw_window(tok, chunk * GROUP + i)) for i in range(GROUP)
        ]
        west[chunk] = jnp.concatenate(parts, 0).astype(BF16)
        halo_copy(chunk).start()
        return 0

    lax.fori_loop(0, chunks, send_west, 0)
    rows_copy.wait_send()
    for load in loads[1:]:
        load.wait()

    score_scale = 32 ** (-0.5) * 1.4426950408889634
    head_of_lane = lax.broadcasted_iota(jnp.int32, (SPAN, 128), 1) // 32
    head_of_row = lax.broadcasted_iota(jnp.int32, (128, 128), 0) // 32
    tail_head = lax.broadcasted_iota(jnp.int32, (128, 64), 1) // 16
    tail_row = lax.broadcasted_iota(jnp.int32, (128, 64), 0) // 32
    sum_row = lax.broadcasted_iota(jnp.int32, (16, 512), 0)
    sum_lane = lax.broadcasted_iota(jnp.int32, (16, 512), 1) // 128
    tail_sum_row = lax.broadcasted_iota(jnp.int32, (16, 64), 0)
    tail_sum_lane = lax.broadcasted_iota(jnp.int32, (16, 64), 1) // 16
    sum_rows = jnp.concatenate(
        [(sum_row == sum_lane).astype(F32), (tail_sum_row == tail_sum_lane).astype(F32)], 1
    ).astype(BF16)
    label_rows = lax.broadcasted_iota(jnp.int32, (128, SPAN), 0).astype(F32)
    eye_row = lax.broadcasted_iota(jnp.int32, (SPAN, SPAN), 0)
    eye = (eye_row == lax.broadcasted_iota(jnp.int32, (SPAN, SPAN), 1)).astype(F32).astype(BF16)

    def stacked(value):
        return jnp.concatenate([value[:128]] * 4 + [value[128:]] * 4, 0)

    def attend_window(window, i):
        base = pl.multiple_of(i * SPAN, 16)
        normed = ns[pl.ds(base, SPAN)]
        value_t = dot_nt(
            w_vt[...], jnp.concatenate([normed[:128]] + [normed[128:]] * 4, 0)
        ).astype(BF16)
        lane_labels = labels[pl.ds(window, 1), :SPAN]
        marks_t = (label_rows == lane_labels).astype(F32).astype(BF16)
        marks = dot_nt(eye, marks_t)
        query_marks = marks.astype(BF16)
        key_marks = stacked(((marks - 1.0) * 1e30).astype(BF16))
        outs = []
        for g in range(HEADS // 4):
            lanes = pl.ds(g * 128, 128)
            query = jnp.concatenate([qs[pl.ds(base, SPAN), lanes], query_marks], 1)
            key = ks[pl.ds(base, SPAN), lanes]
            heads = [jnp.where(head_of_lane == h, key, jnp.zeros_like(key)) for h in range(4)]
            keys = jnp.concatenate([k[:128] for k in heads] + [k[128:] for k in heads], 0)
            keys = jnp.concatenate([keys, key_marks], 1)
            scores = dot_nt(keys, query)
            mains, tails = [], []
            for h in range(4):
                main = scores[128 * h : 128 * h + 128]
                tail = scores[512 + 16 * h : 528 + 16 * h]
                peak = jnp.maximum(
                    jnp.max(main, 0, keepdims=True), jnp.max(tail, 0, keepdims=True)
                )
                mains.append(jnp.exp2((main - peak).astype(BF16)))
                tails.append(jnp.exp2((tail - peak).astype(BF16)))
            weights = jnp.concatenate(mains + tails, 0)
            group_values = value_t[g * 128 : g * 128 + 128]
            main_values = group_values[:, :128]
            tail_values = group_values[:, 128:192]
            parts = [
                jnp.where(head_of_row == h, main_values, jnp.zeros_like(main_values))
                for h in range(4)
            ]
            parts.append(jnp.where(tail_head == tail_row, tail_values, jnp.zeros_like(tail_values)))
            values = jnp.concatenate([jnp.concatenate(parts, 1), sum_rows], 0)
            result = dot(values, weights)
            scale = 1.0 / result[128:136]
            for h in range(4):
                outs.append(result[32 * h : 32 * h + 32] * scale[h : h + 1])
        out_t = jnp.concatenate(outs, 0).astype(BF16)
        wos[pl.ds(pl.multiple_of(i * PADDED, 16), PADDED)] = dot_nt(order[...], out_t).astype(BF16)
        return 0

    def merge(blocks):
        total = sum(jnp.sum(b, -1, keepdims=True) for b in blocks)
        mean = total * (1.0 / 2048)
        blocks = [b - mean for b in blocks]
        spread = sum(jnp.sum(b * b, -1, keepdims=True) for b in blocks) * (1.0 / 2048)
        factor = lax.rsqrt(spread + 1e-05)
        merge_in = jnp.concatenate([(b * factor).astype(BF16) for b in blocks], 1)
        return dot(merge_in, w_merge[...])

    def packed(rows40):
        stacked_lanes = jnp.concatenate([rows40[:, 256 * j : 256 * j + 256] for j in range(4)], 0)
        return dot(pack[...], stacked_lanes.astype(BF16)).astype(BF16)

    def own_copy():
        return pltpu.make_async_copy(
            stage.at[pl.ds(3 * lon, 3)], recv.at[lon], out_recv
        )

    def send_copy(owner):
        return pltpu.make_async_remote_copy(
            src_ref=stage.at[pl.ds(3 * owner, 3)],
            dst_ref=recv.at[lon],
            send_sem=out_send.at[owner],
            recv_sem=out_recv,
            device_id=(lat, owner),
            device_id_type=MESH,
        )

    def own_zero_copy():
        return pltpu.make_async_copy(
            stage.at[pl.ds(1, 2)], recv.at[lon, pl.ds(1, 2)], out_recv
        )

    def send_zero_copy():
        return pltpu.make_async_remote_copy(
            src_ref=stage.at[pl.ds(1, 2)],
            dst_ref=recv.at[lon, pl.ds(1, 2)],
            send_sem=out_send.at[0],
            recv_sem=out_recv,
            device_id=(lat, 0),
            device_id_type=MESH,
        )

    def last_copy():
        return pltpu.make_async_remote_copy(
            src_ref=stage.at[pl.ds(3 * windows, 1)],
            dst_ref=recv.at[lon, pl.ds(0, 1)],
            send_sem=out_send.at[windows],
            recv_sem=out_recv,
            device_id=(next_lat, 0),
            device_id_type=MESH,
        )

    def send(owner):
        @pl.when(owner == lon)
        def _():
            own_copy().start()

        @pl.when(owner != lon)
        def _():
            send_copy(owner).start()

    carry_copy = pltpu.make_async_remote_copy(
        src_ref=carry_send,
        dst_ref=carry_recv,
        send_sem=carry_sems.at[0],
        recv_sem=carry_sems.at[1],
        device_id=(next_lat, lon),
        device_id_type=MESH,
    )

    carry[...] = jnp.zeros_like(carry)
    slot_row = lax.broadcasted_iota(jnp.int32, (GROUP * 40, 512), 0) % 40 < 12

    def chunk_step(step, _):
        chunk = lax.rem(first + step, chunks)
        start = chunk * GROUP

        @pl.when(chunk == chunks - 1)
        def _():
            @pl.when(first_west != chunks - 1)
            def _():
                pass

        halo_copy(chunk).wait_recv()
        for i in range(GROUP):
            own = dot(pick_own[...], raw_window(tok, start + i))
            east = halo[chunk, pl.ds(i * HALF, HALF)].astype(F32) if (i * HALF) % 16 == 0 else None
            if east is None:
                east = halo[chunk, pl.ds(i * HALF - 8, HALF + 8)].astype(F32)[8:]
            value = jnp.concatenate([own, east], 0)
            xs[pl.ds(i * SPAN, SPAN)] = value.astype(BF16)
            ns[pl.ds(i * SPAN, SPAN)] = normalize(value).astype(BF16)
        qs[...] = (dot(ns[...], w_qk[:, :512]) * score_scale).astype(BF16)
        ks[...] = dot(ns[...], w_qk[:, 512:]).astype(BF16)
        lax.fori_loop(0, GROUP, lambda i, _: attend_window(start + i, i), 0)
        residual = jnp.concatenate(
            [dot(order[...], xs[pl.ds(i * SPAN, SPAN)]) for i in range(GROUP)], 0
        )
        updated = (residual + dot(wos[...], w_out[...])).astype(BF16).astype(F32)
        blocks = []
        for p in range(4):
            pieces = [
                updated[PADDED * i + 40 * p : PADDED * i + 40 * p + 40] for i in range(GROUP)
            ]
            block = jnp.concatenate(pieces, 0)
            if p < 2:
                before = jnp.concatenate([carry[pl.ds(40 * p, 40)]] + pieces[:-1], 0)
                carry[pl.ds(40 * p, 40)] = pieces[-1]
                block = jnp.where(slot_row, before, block)
            blocks.append(block)

        @pl.when(step == 0)
        def _():
            for p in range(2):
                odd_save[1, pl.ds(16 * p, 16)] = blocks[2 + p][:16]

        @pl.when(chunk == 0)
        def _():
            for p in range(2):
                odd_save[0, pl.ds(16 * p, 16)] = blocks[2 + p][:16]

        @pl.when(chunk == chunks - 1)
        def _():
            for p in range(2):
                carry_send[pl.ds(16 * p, 16)] = carry[pl.ds(40 * p, 16)].astype(BF16)
            carry_copy.start()

        merged = merge(blocks)
        for i in range(GROUP):
            pieces = packed(merged[40 * i : 40 * i + 40])
            for slot in range(3):
                if i == 0 and slot == 0:
                    stage[3 * start + 1] = pieces[:48]
                else:
                    stage[3 * (start + i) + 1 + slot] = pieces[48 * slot : 48 * slot + 48]
            owner = start + i
            if i == 0:

                @pl.when(jnp.logical_and(step > 0, chunk > 0))
                def _():
                    send(owner)
            else:
                send(owner)

        @pl.when(chunk == chunks - 1)
        def _():
            last_copy().start()

        return 0

    lax.fori_loop(0, chunks, chunk_step, 0)

    carry_copy.wait_recv()
    lat_carry = carry_recv[...].astype(F32)
    blocks = []
    for p in range(2):
        blocks.append(
            jnp.concatenate([lat_carry[16 * p : 16 * p + 16], carry[pl.ds(40 * p, 16)]], 0)
        )
    for p in range(2):
        blocks.append(
            jnp.concatenate([odd_save[0, pl.ds(16 * p, 16)], odd_save[1, pl.ds(16 * p, 16)]], 0)
        )
    merged = merge(blocks)
    zero_rows = jnp.zeros((24, merged.shape[1]), F32)
    stage[1] = packed(jnp.concatenate([merged[:16], zero_rows], 0))[:48]

    @pl.when(lon == 0)
    def _():
        own_zero_copy().start()

    @pl.when(lon != 0)
    def _():
        send_zero_copy().start()

    @pl.when(first != 0)
    def _():
        stage[3 * GROUP * first + 1] = packed(jnp.concatenate([merged[16:], zero_rows], 0))[:48]
        send(GROUP * first)

    def wait_halo(chunk, _):
        halo_copy(chunk).wait_send()
        return 0

    lax.fori_loop(0, chunks, wait_halo, 0)
    carry_copy.wait_send()
    last_copy().wait_send()

    @pl.when(lon != 0)
    def _():
        send_zero_copy().wait_send()

    def wait_send(owner, _):
        @pl.when(owner != lon)
        def _():
            send_copy(owner).wait_send()

        return 0

    lax.fori_loop(1, windows, wait_send, 0)
    pltpu.make_async_copy(recv, recv, out_recv).wait()


def exchange(tokens, labels, w_qkv, w_out, w_merge, n_lat, n_lon):
    levels, rows, cols, channels = tokens.shape
    windows = rows // WIN_LAT
    chunks = windows // GROUP
    vmem = pl.BlockSpec(memory_space=pltpu.VMEM)
    hbm = pl.BlockSpec(memory_space=pl.ANY)
    w_qk = w_qkv[:, : 2 * channels]
    w_vt = w_qkv[:, 2 * channels :].T
    span = GROUP * SPAN
    return pl.pallas_call(
        functools.partial(fused, n_lat, n_lon),
        out_shape=jax.ShapeDtypeStruct((n_lon, 3, 48, 256), BF16),
        in_specs=[hbm] + [vmem] * 5 + [hbm] * 4,
        out_specs=hbm,
        scratch_shapes=[
            pltpu.VMEM((levels, rows + 3, cols, channels), BF16),
            pltpu.VMEM((chunks, GROUP * HALF, channels), BF16),
            pltpu.VMEM((chunks, GROUP * HALF, channels), BF16),
            pltpu.VMEM((3 * windows + 1, 48, 256), BF16),
            pltpu.VMEM((channels, 2 * channels), BF16),
            pltpu.VMEM((channels, channels), BF16),
            pltpu.VMEM((channels, channels), BF16),
            pltpu.VMEM((4 * channels, 2 * channels), BF16),
            pltpu.VMEM((span, channels), BF16),
            pltpu.VMEM((span, channels), BF16),
            pltpu.VMEM((span, channels), BF16),
            pltpu.VMEM((span, channels), BF16),
            pltpu.VMEM((GROUP * PADDED, channels), BF16),
            pltpu.VMEM((80, channels), F32),
            pltpu.VMEM((2, 32, channels), F32),
            pltpu.VMEM((32, channels), BF16),
            pltpu.VMEM((32, channels), BF16),
            pltpu.SemaphoreType.DMA((5,)),
            pltpu.SemaphoreType.DMA((2,)),
            pltpu.SemaphoreType.DMA((chunks,)),
            pltpu.SemaphoreType.DMA((chunks,)),
            pltpu.SemaphoreType.DMA((2,)),
            pltpu.SemaphoreType.DMA((windows + 1,)),
            pltpu.SemaphoreType.DMA,
        ],
        compiler_params=pltpu.CompilerParams(
            collective_id=0, has_side_effects=True, vmem_limit_bytes=56 * 1024 * 1024
        ),
        name="attend_merge_send",
    )(tokens, labels, *tables(), w_qk, w_vt, w_out, w_merge)


def shifted(value, axis, steps):
    count = lax.axis_size(axis)
    pairs = [(source, (source + steps) % count) for source in range(count)]
    return lax.ppermute(value, axis, pairs)


def window_labels(region, n_lat):
    levels, rows, cols = region.shape
    windows = rows // WIN_LAT
    marks = (region * 2).astype(F32)
    after = shifted(marks[:, :3], "lat", -1)
    after = after + (lax.axis_index("lat") == n_lat - 1).astype(F32)
    marks = jnp.concatenate([marks[:, 3:], after], 1)
    halves = marks.reshape(levels, windows, WIN_LAT, 2, WIN_LON // 2)
    halves = halves.transpose(3, 1, 0, 2, 4).reshape(2, windows, HALF)
    east = shifted(halves[0], "lon", -1)
    return jnp.concatenate([halves[1], east, jnp.full((windows, 256 - SPAN), 9.0, F32)], 1)


def arrange(recv, n_lon):
    parts = recv.reshape(n_lon, 3, 4, LEV, 2, 3, 256)
    own, east = parts[..., 0, :, :], parts[..., 1, :, :]
    east = jnp.roll(east, 1, 0)
    parts = jnp.stack([east, own], 4)
    parts = parts.transpose(3, 1, 0, 4, 5, 2, 6)
    return parts.reshape(LEV, 3, n_lon * 6, 1024)


def solution(mesh):
    n_lat, n_lon = mesh.shape["lat"], mesh.shape["lon"]

    def body(tokens, region, w_qkv, w_out, w_merge):
        labels = window_labels(region, n_lat)
        recv = exchange(tokens, labels, w_qkv, w_out, w_merge, n_lat, n_lon)
        return arrange(recv, n_lon)

    in_specs = (P(None, "lat", "lon", None), P(None, "lat", "lon"), P(), P(), P())
    out_specs = P(None, ("lat", "lon"), None, None)
    return jax.shard_map(body, mesh=mesh, in_specs=in_specs, out_specs=out_specs, check_vma=False)
```

```python
import functools

import jax
import jax.numpy as jnp
import numpy as np
from jax import lax
from jax.experimental import pallas as pl
from jax.experimental.pallas import tpu as pltpu
from jax.sharding import PartitionSpec as P

MESH = pl.DeviceIdType.MESH
HEADS = 16
WIN_LAT = 6
WIN_LON = 12
LEV = 2
BLOCK = 192
SPAN = 144
PADDED = 160
GROUP = 4
PICK_STARTS = (0, 1, 1, 2)
PICK_ROWS = (3, 1, 7, 5)
F32 = jnp.float32
BF16 = jnp.bfloat16


def tables():
    pick = np.zeros((SPAN, 2 * BLOCK), np.float32)
    order = np.zeros((PADDED, SPAN), np.float32)
    pack = np.zeros((SPAN, PADDED), np.float32)
    picks = []
    for offset in PICK_ROWS:
        pick = np.zeros((SPAN, 2 * BLOCK), np.float32)
        for line in range(24):
            for row in range(6):
                pick[line * 6 + row, line * 16 + offset + row] = 1
        picks.append(pick)
    window_rows = ((5, 1, 3), (0, 2, 4))
    for odd in range(2):
        for right in range(2):
            block = odd * 2 + right
            for slot in range(3):
                for lev in range(LEV):
                    for patch in range(6):
                        half, col = divmod(patch, 3)
                        line = half * 12 + lev * 6 + 2 * col + right
                        token = line * 6 + window_rows[odd][slot]
                        order[block * 40 + slot * 12 + lev * 6 + patch, token] = 1
    for slot in range(3):
        for lanes in range(4):
            for place in range(12):
                pack[slot * 48 + lanes * 12 + place, lanes * 40 + slot * 12 + place] = 1
    return [jnp.asarray(t, BF16) for t in (np.stack(picks), order, pack)]


def arrange_table():
    table = np.zeros((384, 432), np.float32)
    for lev in range(LEV):
        for lanes in range(4):
            for col in range(48):
                device, place = divmod(col, 6)
                source, patch = (device, 3 + place) if place < 3 else (device + 1, place - 3)
                piece = source * 48 + lanes * 12 + lev * 6 + patch
                table[(lev * 4 + lanes) * 48 + col, piece] = 1
    return jnp.asarray(table, BF16)


def dot(a, b):
    return jnp.dot(a, b, preferred_element_type=F32)


def dot_nt(a, b):
    return lax.dot_general(a, b, (((1,), (1,)), ((), ())), preferred_element_type=F32)


def normalize(values):
    center = values - jnp.mean(values, -1, keepdims=True)
    spread = jnp.mean(center * center, -1, keepdims=True)
    return center * lax.rsqrt(spread + 1e-05)


def fused(
    n_lat,
    n_lon,
    tokens,
    region,
    pick,
    order,
    pack,
    w_qkv_hbm,
    w_out_hbm,
    w_merge_hbm,
    recv,
    own,
    east,
    own_region,
    east_region,
    own_next,
    east_next,
    own_marks,
    east_marks,
    stage,
    w_qk,
    w_v,
    w_vt,
    w_out,
    w_merge,
    xs,
    ns,
    ms,
    qs,
    ks,
    wos,
    carry,
    odd_save,
    carry_send,
    carry_recv,
    load_sems,
    row_send,
    row_recv,
    halo_send,
    halo_recv,
    carry_sems,
    out_send,
    out_recv,
):
    lat = lax.axis_index("lat")
    lon = lax.axis_index("lon")
    next_lat = lax.rem(lat + 1, n_lat)
    prev_lat = lax.rem(lat + n_lat - 1, n_lat)
    west_lon = lax.rem(lon + n_lon - 1, n_lon)
    east_lon = lax.rem(lon + 1, n_lon)
    rows = tokens.shape[2] * 8
    channels = tokens.shape[4]
    windows = rows // WIN_LAT
    chunks = windows // GROUP
    pairs = chunks // 2
    blocks16 = rows // 16
    first_pair = lax.rem((lon * pairs) // n_lon, pairs)
    first = 2 * first_pair
    first_west = lax.rem((west_lon * pairs) // n_lon, pairs)

    loads = [
        pltpu.make_async_copy(tokens.at[:, 6:12], own.at[:, :, : rows // 8], load_sems.at[0]),
        pltpu.make_async_copy(region.at[6:12], own_region, load_sems.at[1]),
        pltpu.make_async_copy(w_qkv_hbm.at[:, : 2 * channels], w_qk, load_sems.at[2]),
        pltpu.make_async_copy(w_qkv_hbm.at[:, 2 * channels :], w_v, load_sems.at[3]),
        pltpu.make_async_copy(w_out_hbm, w_out, load_sems.at[4]),
        pltpu.make_async_copy(w_merge_hbm, w_merge, load_sems.at[5]),
    ]
    for load in loads:
        load.start()

    barrier = pltpu.get_barrier_semaphore()

    def greet(step, _):
        other = lax.rem(lon + step, n_lon)
        pl.semaphore_signal(barrier, inc=1, device_id=(lat, other), device_id_type=MESH)
        return 0

    lax.fori_loop(1, n_lon, greet, 0)
    pl.semaphore_signal(barrier, inc=1, device_id=(prev_lat, lon), device_id_type=MESH)
    pl.semaphore_signal(barrier, inc=1, device_id=(next_lat, lon), device_id_type=MESH)
    pl.semaphore_signal(barrier, inc=1, device_id=(next_lat, east_lon), device_id_type=MESH)

    @pl.when(lon == 0)
    def _():
        def greet_before(other, _):
            pl.semaphore_signal(barrier, inc=1, device_id=(prev_lat, other), device_id_type=MESH)
            return 0

        lax.fori_loop(0, n_lon, greet_before, 0)

    pl.semaphore_wait(barrier, n_lon + 3)

    def remote(source, target, send_sem, recv_sem, device):
        return pltpu.make_async_remote_copy(
            src_ref=source,
            dst_ref=target,
            send_sem=send_sem,
            recv_sem=recv_sem,
            device_id=device,
            device_id_type=MESH,
        )

    def halo_copy(block):
        part = pl.ds(block * 2, 2)
        return remote(
            tokens.at[:, 0:6, part],
            east.at[:, :, part],
            halo_send.at[block],
            halo_recv.at[block],
            (lat, west_lon),
        )

    def send_west(step, _):
        halo_copy(lax.rem(3 * first_west + step, blocks16)).start()
        return 0

    next_rows = pl.ds(rows // 8, 1)
    ahead = [
        remote(region.at[0:6], east_region, row_send.at[0], row_recv.at[0], (lat, west_lon)),
        remote(
            region.at[6:12, :, :128], own_next, row_send.at[1], row_recv.at[1], (prev_lat, lon)
        ),
        remote(
            region.at[0:6, :, :128],
            east_next,
            row_send.at[2],
            row_recv.at[2],
            (prev_lat, west_lon),
        ),
        remote(
            tokens.at[:, 6:12, 0:1],
            own.at[:, :, next_rows],
            row_send.at[3],
            row_recv.at[3],
            (prev_lat, lon),
        ),
        remote(
            tokens.at[:, 0:6, 0:1],
            east.at[:, :, next_rows],
            row_send.at[4],
            row_recv.at[4],
            (prev_lat, west_lon),
        ),
    ]
    for copy in ahead[:3]:
        copy.start()
    lax.fori_loop(0, 4, send_west, 0)
    for copy in ahead[3:]:
        copy.start()
    lax.fori_loop(4, blocks16, send_west, 0)

    def eye(size):
        row = lax.broadcasted_iota(jnp.int32, (size, size), 0)
        return (row == lax.broadcasted_iota(jnp.int32, (size, size), 1)).astype(F32).astype(BF16)

    def one_hot(lane_labels):
        label = lax.broadcasted_iota(jnp.int32, (128, lane_labels.shape[1]), 0)
        return (label == lane_labels).astype(F32).astype(BF16)

    pole = (lat == n_lat - 1).astype(jnp.int32)
    row_eye = eye(rows)
    next_eye = eye(128)[:8]

    def mark_half(here, after, marks):
        def mark_column(col, _):
            for lev in range(LEV):
                labels = here[col, lev : lev + 1] * 2
                marks[lev, col, pl.ds(0, rows // 8)] = (
                    dot_nt(row_eye, one_hot(labels)).astype(BF16).reshape(rows // 8, 8, 128)
                )
                labels = after[col, lev : lev + 1] * 2 + pole
                marks[lev, col, rows // 8] = dot_nt(next_eye, one_hot(labels)).astype(BF16)
            return 0

        lax.fori_loop(0, 6, mark_column, 0)

    loads[1].wait()
    ahead[1].wait_recv()
    mark_half(own_region, own_next, own_marks)
    loads[3].wait()
    w_vt[...] = dot_nt(eye(channels), w_v[...]).astype(BF16)
    ahead[0].wait_recv()
    ahead[2].wait_recv()
    mark_half(east_region, east_next, east_marks)
    for load in (loads[0], loads[2], loads[4], loads[5]):
        load.wait()

    score_scale = 32 ** (-0.5) * 1.4426950408889634
    head_of_lane = lax.broadcasted_iota(jnp.int32, (SPAN, 128), 1) // 32
    head_of_row = lax.broadcasted_iota(jnp.int32, (128, 128), 0) // 32
    tail_head = lax.broadcasted_iota(jnp.int32, (128, 64), 1) // 16
    tail_row = lax.broadcasted_iota(jnp.int32, (128, 64), 0) // 32
    sum_row = lax.broadcasted_iota(jnp.int32, (16, 512), 0)
    sum_lane = lax.broadcasted_iota(jnp.int32, (16, 512), 1) // 128
    tail_sum_row = lax.broadcasted_iota(jnp.int32, (16, 64), 0)
    tail_sum_lane = lax.broadcasted_iota(jnp.int32, (16, 64), 1) // 16
    sum_rows = jnp.concatenate(
        [(sum_row == sum_lane).astype(F32), (tail_sum_row == tail_sum_lane).astype(F32)], 1
    ).astype(BF16)
    def stacked(value):
        return jnp.concatenate([value[:128]] * 4 + [value[128:]] * 4, 0)

    def window_parts(i):
        normed = ns[pl.ds(i * SPAN, SPAN)]
        value_t = dot_nt(
            w_vt[...], jnp.concatenate([normed[:128]] + [normed[128:]] * 4, 0)
        ).astype(BF16)
        marks = ms[pl.ds(i * SPAN, SPAN)]
        key_marks = stacked(((marks.astype(F32) - 1.0) * 1e30).astype(BF16))
        return value_t, marks, key_marks

    def scores_of(i, g, parts):
        base = i * SPAN
        lanes = pl.ds(g * 128, 128)
        query = jnp.concatenate([qs[pl.ds(base, SPAN), lanes], parts[1]], 1)
        key = ks[pl.ds(base, SPAN), lanes]
        heads = [jnp.where(head_of_lane == h, key, jnp.zeros_like(key)) for h in range(4)]
        keys = jnp.concatenate([k[:128] for k in heads] + [k[128:] for k in heads], 0)
        return dot_nt(jnp.concatenate([keys, parts[2]], 1), query)

    def weights_of(scores):
        mains, tails = [], []
        for h in range(4):
            main = scores[128 * h : 128 * h + 128]
            tail = scores[512 + 16 * h : 528 + 16 * h]
            peak = jnp.maximum(jnp.max(main, 0, keepdims=True), jnp.max(tail, 0, keepdims=True))
            mains.append(jnp.exp2((main - peak).astype(BF16)))
            tails.append(jnp.exp2((tail - peak).astype(BF16)))
        return jnp.concatenate(mains + tails, 0)

    def outs_of(g, parts, weights):
        group_values = parts[0][g * 128 : g * 128 + 128]
        main_values = group_values[:, :128]
        tail_values = group_values[:, 128:192]
        blocks = [
            jnp.where(head_of_row == h, main_values, jnp.zeros_like(main_values)) for h in range(4)
        ]
        blocks.append(jnp.where(tail_head == tail_row, tail_values, jnp.zeros_like(tail_values)))
        values = jnp.concatenate([jnp.concatenate(blocks, 1), sum_rows], 0)
        result = dot(values, weights)
        scale = 1.0 / result[128:136]
        return [result[32 * h : 32 * h + 32] * scale[h : h + 1] for h in range(4)]

    def attend_chunk():
        groups = HEADS // 4
        count = GROUP * groups
        parts, scores, weights, outs = {}, {}, {}, {i: [] for i in range(GROUP)}
        for t in range(count + 2):
            if t < count:
                i, g = divmod(t, groups)
                if g == 0:
                    parts[i] = window_parts(i)
                scores[t] = scores_of(i, g, parts[i])
            if 0 <= t - 2 < count:
                i, g = divmod(t - 2, groups)
                outs[i] += outs_of(g, parts[i], weights.pop(t - 2))
                if g == groups - 1:
                    out_t = jnp.concatenate(outs.pop(i), 0).astype(BF16)
                    wos[pl.ds(i * PADDED, PADDED)] = dot_nt(order[...], out_t).astype(BF16)
            if 0 <= t - 1 < count:
                weights[t - 1] = weights_of(scores.pop(t - 1))

    def merge(blocks):
        total = sum(jnp.sum(b, -1, keepdims=True) for b in blocks)
        mean = total * (1.0 / 2048)
        blocks = [b - mean for b in blocks]
        spread = sum(jnp.sum(b * b, -1, keepdims=True) for b in blocks) * (1.0 / 2048)
        factor = lax.rsqrt(spread + 1e-05)
        merge_in = jnp.concatenate([(b * factor).astype(BF16) for b in blocks], 1)
        return dot(merge_in, w_merge[...])

    def packed(rows40):
        stacked_lanes = jnp.concatenate([rows40[:, 256 * j : 256 * j + 256] for j in range(4)], 0)
        return dot(pack[...], stacked_lanes.astype(BF16)).astype(BF16)

    def own_copy():
        return pltpu.make_async_copy(
            stage.at[pl.ds(3 * lon, 3)], recv.at[lon], out_recv
        )

    def send_copy(owner):
        return pltpu.make_async_remote_copy(
            src_ref=stage.at[pl.ds(3 * owner, 3)],
            dst_ref=recv.at[lon],
            send_sem=out_send.at[owner],
            recv_sem=out_recv,
            device_id=(lat, owner),
            device_id_type=MESH,
        )

    def own_zero_copy():
        return pltpu.make_async_copy(
            stage.at[pl.ds(1, 2)], recv.at[lon, pl.ds(1, 2)], out_recv
        )

    def send_zero_copy():
        return pltpu.make_async_remote_copy(
            src_ref=stage.at[pl.ds(1, 2)],
            dst_ref=recv.at[lon, pl.ds(1, 2)],
            send_sem=out_send.at[0],
            recv_sem=out_recv,
            device_id=(lat, 0),
            device_id_type=MESH,
        )

    def last_copy():
        return pltpu.make_async_remote_copy(
            src_ref=stage.at[pl.ds(3 * windows, 1)],
            dst_ref=recv.at[lon, pl.ds(0, 1)],
            send_sem=out_send.at[windows],
            recv_sem=out_recv,
            device_id=(next_lat, 0),
            device_id_type=MESH,
        )

    def send(owner):
        @pl.when(owner == lon)
        def _():
            own_copy().start()

        @pl.when(owner != lon)
        def _():
            send_copy(owner).start()

    carry_copy = pltpu.make_async_remote_copy(
        src_ref=carry_send,
        dst_ref=carry_recv,
        send_sem=carry_sems.at[0],
        recv_sem=carry_sems.at[1],
        device_id=(next_lat, lon),
        device_id_type=MESH,
    )

    carry[...] = jnp.zeros_like(carry)
    slot_row = lax.broadcasted_iota(jnp.int32, (GROUP * 40, 512), 0) % 40 < 12

    def chunk_step(step, _):
        chunk = lax.rem(first + step, chunks)
        start = chunk * GROUP

        pair = chunk // 2
        even = chunk == 2 * pair

        @pl.when(jnp.logical_and(even, jnp.logical_or(step == 0, pair == 0)))
        def _():
            halo_copy(3 * pair).wait_recv()

        @pl.when(even)
        def _():
            halo_copy(3 * pair + 1).wait_recv()

        @pl.when(jnp.logical_not(even))
        def _():
            halo_copy(3 * pair + 2).wait_recv()

            @pl.when(jnp.logical_and(pair != pairs - 1, pair + 1 != first_pair))
            def _():
                halo_copy(3 * pair + 3).wait_recv()

            @pl.when(pair == pairs - 1)
            def _():
                ahead[3].wait_recv()
                ahead[4].wait_recv()

        for i in range(GROUP):
            part = pl.ds(3 * chunk + PICK_STARTS[i], 2)
            raw = [
                jnp.concatenate(
                    [value[:, :, part].reshape(BLOCK, channels), marks[:, :, part].reshape(BLOCK, 128)],
                    1,
                )
                for value, marks in ((own, own_marks), (east, east_marks))
            ]
            value = dot(pick[i], jnp.concatenate(raw, 0))
            ms[pl.ds(i * SPAN, SPAN)] = value[:, channels:].astype(BF16)
            value = value[:, :channels]
            xs[pl.ds(i * SPAN, SPAN)] = value.astype(BF16)
            ns[pl.ds(i * SPAN, SPAN)] = normalize(value).astype(BF16)
        qs[...] = (dot(ns[...], w_qk[:, :512]) * score_scale).astype(BF16)
        ks[...] = dot(ns[...], w_qk[:, 512:]).astype(BF16)
        attend_chunk()
        residual = jnp.concatenate(
            [dot(order[...], xs[pl.ds(i * SPAN, SPAN)]) for i in range(GROUP)], 0
        )
        updated = (residual + dot(wos[...], w_out[...])).astype(BF16).astype(F32)
        blocks = []
        for p in range(4):
            pieces = [
                updated[PADDED * i + 40 * p : PADDED * i + 40 * p + 40] for i in range(GROUP)
            ]
            block = jnp.concatenate(pieces, 0)
            if p < 2:
                before = jnp.concatenate([carry[pl.ds(40 * p, 40)]] + pieces[:-1], 0)
                carry[pl.ds(40 * p, 40)] = pieces[-1]
                block = jnp.where(slot_row, before, block)
            blocks.append(block)

        @pl.when(step == 0)
        def _():
            for p in range(2):
                odd_save[1, pl.ds(16 * p, 16)] = blocks[2 + p][:16]

        @pl.when(chunk == 0)
        def _():
            for p in range(2):
                odd_save[0, pl.ds(16 * p, 16)] = blocks[2 + p][:16]

        @pl.when(chunk == chunks - 1)
        def _():
            for p in range(2):
                carry_send[pl.ds(16 * p, 16)] = carry[pl.ds(40 * p, 16)].astype(BF16)
            carry_copy.start()

        merged = merge(blocks)
        for i in range(GROUP):
            pieces = packed(merged[40 * i : 40 * i + 40])
            for slot in range(3):
                stage[3 * (start + i) + 1 + slot] = pieces[48 * slot : 48 * slot + 48]
            owner = start + i
            if i == 0:

                @pl.when(jnp.logical_and(step > 0, chunk > 0))
                def _():
                    send(owner)
            else:
                send(owner)

        @pl.when(chunk == chunks - 1)
        def _():
            last_copy().start()

        return 0

    lax.fori_loop(0, chunks, chunk_step, 0)

    carry_copy.wait_recv()
    lat_carry = carry_recv[...].astype(F32)
    blocks = []
    for p in range(2):
        blocks.append(
            jnp.concatenate([lat_carry[16 * p : 16 * p + 16], carry[pl.ds(40 * p, 16)]], 0)
        )
    for p in range(2):
        blocks.append(
            jnp.concatenate([odd_save[0, pl.ds(16 * p, 16)], odd_save[1, pl.ds(16 * p, 16)]], 0)
        )
    merged = merge(blocks)
    zero_rows = jnp.zeros((24, merged.shape[1]), F32)
    stage[1] = packed(jnp.concatenate([merged[:16], zero_rows], 0))[:48]

    @pl.when(lon == 0)
    def _():
        own_zero_copy().start()

    @pl.when(lon != 0)
    def _():
        send_zero_copy().start()

    @pl.when(first != 0)
    def _():
        stage[3 * GROUP * first + 1] = packed(jnp.concatenate([merged[16:], zero_rows], 0))[:48]
        send(GROUP * first)

    def wait_halo(block, _):
        halo_copy(block).wait_send()
        return 0

    lax.fori_loop(0, blocks16, wait_halo, 0)
    for copy in ahead:
        copy.wait_send()
    carry_copy.wait_send()
    last_copy().wait_send()

    @pl.when(lon != 0)
    def _():
        send_zero_copy().wait_send()

    def wait_send(owner, _):
        @pl.when(owner != lon)
        def _():
            send_copy(owner).wait_send()

        return 0

    lax.fori_loop(1, windows, wait_send, 0)
    pltpu.make_async_copy(recv, recv, out_recv).wait()


def exchange(tokens, region, w_qkv, w_out, w_merge, n_lat, n_lon):
    levels, cols, tiles, _, channels = tokens.shape
    rows = tiles * 8
    windows = rows // WIN_LAT
    vmem = pl.BlockSpec(memory_space=pltpu.VMEM)
    hbm = pl.BlockSpec(memory_space=pl.ANY)
    span = GROUP * SPAN
    half = cols // 2
    return pl.pallas_call(
        functools.partial(fused, n_lat, n_lon),
        out_shape=jax.ShapeDtypeStruct((n_lon, 3, 48, 256), BF16),
        in_specs=[hbm] * 2 + [vmem] * 3 + [hbm] * 3,
        out_specs=hbm,
        scratch_shapes=[
            pltpu.VMEM((levels, half, tiles + 1, 8, channels), BF16),
            pltpu.VMEM((levels, half, tiles + 1, 8, channels), BF16),
            pltpu.VMEM((half, levels, rows), jnp.int32),
            pltpu.VMEM((half, levels, rows), jnp.int32),
            pltpu.VMEM((half, levels, 128), jnp.int32),
            pltpu.VMEM((half, levels, 128), jnp.int32),
            pltpu.VMEM((levels, half, tiles + 1, 8, 128), BF16),
            pltpu.VMEM((levels, half, tiles + 1, 8, 128), BF16),
            pltpu.VMEM((3 * windows + 1, 48, 256), BF16),
            pltpu.VMEM((channels, 2 * channels), BF16),
            pltpu.VMEM((channels, channels), BF16),
            pltpu.VMEM((channels, channels), BF16),
            pltpu.VMEM((channels, channels), BF16),
            pltpu.VMEM((4 * channels, 2 * channels), BF16),
            pltpu.VMEM((span, channels), BF16),
            pltpu.VMEM((span, channels), BF16),
            pltpu.VMEM((span, 128), BF16),
            pltpu.VMEM((span, channels), BF16),
            pltpu.VMEM((span, channels), BF16),
            pltpu.VMEM((GROUP * PADDED, channels), BF16),
            pltpu.VMEM((80, channels), F32),
            pltpu.VMEM((2, 32, channels), F32),
            pltpu.VMEM((32, channels), BF16),
            pltpu.VMEM((32, channels), BF16),
            pltpu.SemaphoreType.DMA((6,)),
            pltpu.SemaphoreType.DMA((5,)),
            pltpu.SemaphoreType.DMA((5,)),
            pltpu.SemaphoreType.DMA((rows // 16,)),
            pltpu.SemaphoreType.DMA((rows // 16,)),
            pltpu.SemaphoreType.DMA((2,)),
            pltpu.SemaphoreType.DMA((windows + 1,)),
            pltpu.SemaphoreType.DMA,
        ],
        compiler_params=pltpu.CompilerParams(
            collective_id=0, has_side_effects=True, vmem_limit_bytes=56 * 1024 * 1024
        ),
        name="attend_merge_send",
    )(tokens, region, *tables(), w_qkv, w_out, w_merge)


def place(table, pieces, out):
    sources = pieces.shape[0]
    for group in range(sources // 8):
        before = pieces[(8 * group + sources - 1) % sources, 0]
        here = pieces[8 * group : 8 * group + 8, 0].reshape(384, 256)
        columns = dot(table[...], jnp.concatenate([before, here], 0)).astype(BF16)
        for lev in range(LEV):
            for lanes in range(4):
                at = (lev * 4 + lanes) * 48
                out[lev, 0, 48 * group : 48 * group + 48, 256 * lanes : 256 * lanes + 256] = (
                    columns[at : at + 48]
                )


def arrange(recv):
    n_lon = recv.shape[0]
    return pl.pallas_call(
        place,
        grid=(3,),
        out_shape=jax.ShapeDtypeStruct((LEV, 3, n_lon * 6, 1024), BF16),
        in_specs=[
            pl.BlockSpec((384, 432), lambda row: (0, 0)),
            pl.BlockSpec((n_lon, 1, 48, 256), lambda row: (0, row, 0, 0)),
        ],
        out_specs=pl.BlockSpec((LEV, 1, n_lon * 6, 1024), lambda row: (0, row, 0, 0)),
        name="place_columns",
    )(arrange_table(), recv)


def solution(mesh):
    n_lat, n_lon = mesh.shape["lat"], mesh.shape["lon"]

    def body(tokens, region, w_qkv, w_out, w_merge):
        levels, rows, cols, channels = tokens.shape
        by_column = tokens.transpose(0, 2, 1, 3).reshape(levels, cols, rows // 8, 8, channels)
        recv = exchange(
            by_column, region.transpose(2, 0, 1), w_qkv, w_out, w_merge, n_lat, n_lon
        )
        return arrange(recv)

    in_specs = (P(None, "lat", "lon", None), P(None, "lat", "lon"), P(), P(), P())
    out_specs = P(None, ("lat", "lon"), None, None)
    return jax.shard_map(body, mesh=mesh, in_specs=in_specs, out_specs=out_specs, check_vma=False)
```

```python
import functools

import jax
import jax.numpy as jnp
import numpy as np
from jax import lax
from jax.experimental import pallas as pl
from jax.experimental.pallas import tpu as pltpu
from jax.sharding import PartitionSpec as P

MESH = pl.DeviceIdType.MESH
HEADS = 16
WIN_LAT = 6
WIN_LON = 12
LEV = 2
BLOCK = 192
SPAN = 144
PADDED = 160
GROUP = 4
PICK_STARTS = (0, 1, 1, 2)
PICK_ROWS = (3, 1, 7, 5)
F32 = jnp.float32
BF16 = jnp.bfloat16


def tables():
    pick = np.zeros((SPAN, 2 * BLOCK), np.float32)
    order = np.zeros((PADDED, SPAN), np.float32)
    pack = np.zeros((SPAN // 2, PADDED // 2), np.float32)
    picks = []
    for offset in PICK_ROWS:
        pick = np.zeros((SPAN, 2 * BLOCK), np.float32)
        for line in range(24):
            for row in range(6):
                pick[line * 6 + row, line * 16 + offset + row] = 1
        picks.append(pick)
    window_rows = ((5, 1, 3), (0, 2, 4))
    for odd in range(2):
        for right in range(2):
            block = odd * 2 + right
            for slot in range(3):
                for lev in range(LEV):
                    for patch in range(6):
                        half, col = divmod(patch, 3)
                        line = half * 12 + lev * 6 + 2 * col + right
                        token = line * 6 + window_rows[odd][slot]
                        order[block * 40 + slot * 12 + lev * 6 + patch, token] = 1
    for slot in range(3):
        for lanes in range(2):
            for place in range(12):
                pack[slot * 24 + lanes * 12 + place, lanes * 40 + slot * 12 + place] = 1
    return [jnp.asarray(t, BF16) for t in (np.stack(picks), order, pack)]


def arrange_table():
    table = np.zeros((192, 216), np.float32)
    for lev in range(LEV):
        for lanes in range(2):
            for col in range(48):
                device, place = divmod(col, 6)
                source, patch = (device, 3 + place) if place < 3 else (device + 1, place - 3)
                piece = source * 24 + lanes * 12 + lev * 6 + patch
                table[(lev * 2 + lanes) * 48 + col, piece] = 1
    return jnp.asarray(table, BF16)


def dot(a, b):
    return jnp.dot(a, b, preferred_element_type=F32)


def dot_nt(a, b):
    return lax.dot_general(a, b, (((1,), (1,)), ((), ())), preferred_element_type=F32)


def normalize(values):
    center = values - jnp.mean(values, -1, keepdims=True)
    spread = jnp.mean(center * center, -1, keepdims=True)
    return center * lax.rsqrt(spread + 1e-05)


def fused(
    n_lat,
    n_lon,
    tokens,
    region,
    pick,
    order,
    pack,
    w_qkv_hbm,
    w_out_hbm,
    w_merge_hbm,
    recv,
    own,
    east,
    own_region,
    east_region,
    own_next,
    east_next,
    own_marks,
    east_marks,
    stage,
    w_qk,
    w_v,
    w_vt,
    w_out,
    w_merge,
    xs,
    ns,
    ms,
    qs,
    ks,
    wos,
    carry,
    odd_save,
    carry_send,
    carry_recv,
    load_sems,
    row_send,
    row_recv,
    halo_send,
    halo_recv,
    carry_sems,
    out_send,
    out_recv,
):
    lat = lax.axis_index("lat")
    lon = lax.axis_index("lon")
    next_lat = lax.rem(lat + 1, n_lat)
    prev_lat = lax.rem(lat + n_lat - 1, n_lat)
    west_lon = lax.rem(lon + n_lon - 1, n_lon)
    east_lon = lax.rem(lon + 1, n_lon)
    rows = tokens.shape[2] * 8
    channels = tokens.shape[4]
    windows = rows // WIN_LAT
    chunks = windows // GROUP

    def first_chunk(place):
        return (place // 8) * (chunks // 4)

    first = first_chunk(lon)
    first_west = first_chunk(west_lon)

    loads = [
        pltpu.make_async_copy(tokens.at[:, 6:12], own.at[:, :, : rows // 8], load_sems.at[0]),
        pltpu.make_async_copy(region.at[6:12], own_region, load_sems.at[1]),
        pltpu.make_async_copy(w_qkv_hbm.at[:, : 2 * channels], w_qk, load_sems.at[2]),
        pltpu.make_async_copy(w_qkv_hbm.at[:, 2 * channels :], w_v, load_sems.at[3]),
        pltpu.make_async_copy(w_out_hbm, w_out, load_sems.at[4]),
        pltpu.make_async_copy(w_merge_hbm, w_merge, load_sems.at[5]),
    ]
    for load in loads:
        load.start()

    barrier = pltpu.get_barrier_semaphore()

    def greet(step, _):
        other = lax.rem(lon + step, n_lon)
        pl.semaphore_signal(barrier, inc=1, device_id=(lat, other), device_id_type=MESH)
        return 0

    lax.fori_loop(1, n_lon, greet, 0)
    pl.semaphore_signal(barrier, inc=1, device_id=(prev_lat, lon), device_id_type=MESH)
    pl.semaphore_signal(barrier, inc=1, device_id=(next_lat, lon), device_id_type=MESH)
    pl.semaphore_signal(barrier, inc=1, device_id=(next_lat, east_lon), device_id_type=MESH)

    @pl.when(lon == 0)
    def _():
        def greet_before(other, _):
            pl.semaphore_signal(barrier, inc=1, device_id=(prev_lat, other), device_id_type=MESH)
            return 0

        lax.fori_loop(0, n_lon, greet_before, 0)

    pl.semaphore_wait(barrier, n_lon + 3)

    def remote(source, target, send_sem, recv_sem, device):
        return pltpu.make_async_remote_copy(
            src_ref=source,
            dst_ref=target,
            send_sem=send_sem,
            recv_sem=recv_sem,
            device_id=device,
            device_id_type=MESH,
        )

    def halo_copy(chunk, start, count):
        part = pl.ds(start, count)
        return remote(
            tokens.at[:, 0:6, part],
            east.at[:, :, part],
            halo_send.at[chunk],
            halo_recv.at[chunk],
            (lat, west_lon),
        )

    def halo_case(chunk, start_chunk, act):
        head = jnp.logical_or(chunk == start_chunk, chunk == 0)
        short = jnp.logical_or(chunk == chunks - 1, chunk + 1 == start_chunk)
        for is_head in (False, True):
            for is_short in (False, True):

                @pl.when(jnp.logical_and(head == is_head, short == is_short))
                def _():
                    count = 3 + int(is_head) - int(is_short)
                    act(halo_copy(chunk, 3 * chunk + 1 - int(is_head), count))

    def send_west(step, _):
        halo_case(lax.rem(first_west + step, chunks), first_west, lambda copy: copy.start())
        return 0

    next_rows = pl.ds(rows // 8, 1)
    ahead = [
        remote(region.at[0:6], east_region, row_send.at[0], row_recv.at[0], (lat, west_lon)),
        remote(
            region.at[6:12, :, :128], own_next, row_send.at[1], row_recv.at[1], (prev_lat, lon)
        ),
        remote(
            region.at[0:6, :, :128],
            east_next,
            row_send.at[2],
            row_recv.at[2],
            (prev_lat, west_lon),
        ),
        remote(
            tokens.at[:, 6:12, 0:1],
            own.at[:, :, next_rows],
            row_send.at[3],
            row_recv.at[3],
            (prev_lat, lon),
        ),
        remote(
            tokens.at[:, 0:6, 0:1],
            east.at[:, :, next_rows],
            row_send.at[4],
            row_recv.at[4],
            (prev_lat, west_lon),
        ),
    ]
    for copy in ahead[:3]:
        copy.start()
    lax.fori_loop(0, 2, send_west, 0)
    for copy in ahead[3:]:
        copy.start()
    lax.fori_loop(2, chunks, send_west, 0)

    def eye(size):
        row = lax.broadcasted_iota(jnp.int32, (size, size), 0)
        return (row == lax.broadcasted_iota(jnp.int32, (size, size), 1)).astype(F32).astype(BF16)

    def one_hot(lane_labels):
        label = lax.broadcasted_iota(jnp.int32, (128, lane_labels.shape[1]), 0)
        return (label == lane_labels).astype(F32).astype(BF16)

    pole = (lat == n_lat - 1).astype(jnp.int32)
    row_eye = eye(rows)
    next_eye = eye(128)[:8]

    def mark_half(here, after, marks):
        def mark_column(col, _):
            for lev in range(LEV):
                labels = here[col, lev : lev + 1] * 2
                marks[lev, col, pl.ds(0, rows // 8)] = (
                    dot_nt(row_eye, one_hot(labels)).astype(BF16).reshape(rows // 8, 8, 128)
                )
                labels = after[col, lev : lev + 1] * 2 + pole
                marks[lev, col, rows // 8] = dot_nt(next_eye, one_hot(labels)).astype(BF16)
            return 0

        lax.fori_loop(0, 6, mark_column, 0)

    loads[1].wait()
    ahead[1].wait_recv()
    mark_half(own_region, own_next, own_marks)
    loads[3].wait()
    w_vt[...] = dot_nt(eye(channels), w_v[...]).astype(BF16)
    ahead[0].wait_recv()
    ahead[2].wait_recv()
    mark_half(east_region, east_next, east_marks)
    for load in (loads[0], loads[2], loads[4], loads[5]):
        load.wait()

    score_scale = 32 ** (-0.5) * 1.4426950408889634
    head_of_lane = lax.broadcasted_iota(jnp.int32, (SPAN, 128), 1) // 32
    head_of_row = lax.broadcasted_iota(jnp.int32, (128, 128), 0) // 32
    tail_head = lax.broadcasted_iota(jnp.int32, (128, 64), 1) // 16
    tail_row = lax.broadcasted_iota(jnp.int32, (128, 64), 0) // 32
    sum_row = lax.broadcasted_iota(jnp.int32, (16, 512), 0)
    sum_lane = lax.broadcasted_iota(jnp.int32, (16, 512), 1) // 128
    tail_sum_row = lax.broadcasted_iota(jnp.int32, (16, 64), 0)
    tail_sum_lane = lax.broadcasted_iota(jnp.int32, (16, 64), 1) // 16
    sum_rows = jnp.concatenate(
        [(sum_row == sum_lane).astype(F32), (tail_sum_row == tail_sum_lane).astype(F32)], 1
    ).astype(BF16)
    def stacked(value):
        return jnp.concatenate([value[:128]] * 4 + [value[128:]] * 4, 0)

    def window_parts(i):
        normed = ns[pl.ds(i * SPAN, SPAN)]
        value_t = dot_nt(
            w_vt[...], jnp.concatenate([normed[:128]] + [normed[128:]] * 4, 0)
        ).astype(BF16)
        marks = ms[pl.ds(i * SPAN, SPAN)]
        key_marks = stacked(((marks.astype(F32) - 1.0) * 1e30).astype(BF16))
        return value_t, marks, key_marks

    def scores_of(i, g, parts):
        base = i * SPAN
        lanes = pl.ds(g * 128, 128)
        query = jnp.concatenate([qs[pl.ds(base, SPAN), lanes], parts[1]], 1)
        key = ks[pl.ds(base, SPAN), lanes]
        heads = [jnp.where(head_of_lane == h, key, jnp.zeros_like(key)) for h in range(4)]
        keys = jnp.concatenate([k[:128] for k in heads] + [k[128:] for k in heads], 0)
        return dot_nt(jnp.concatenate([keys, parts[2]], 1), query)

    def weights_of(scores):
        mains, tails = [], []
        for h in range(4):
            main = scores[128 * h : 128 * h + 128]
            tail = scores[512 + 16 * h : 528 + 16 * h]
            peak = jnp.maximum(jnp.max(main, 0, keepdims=True), jnp.max(tail, 0, keepdims=True))
            mains.append(jnp.exp2((main - peak).astype(BF16)))
            tails.append(jnp.exp2((tail - peak).astype(BF16)))
        return jnp.concatenate(mains + tails, 0)

    def outs_of(g, parts, weights):
        group_values = parts[0][g * 128 : g * 128 + 128]
        main_values = group_values[:, :128]
        tail_values = group_values[:, 128:192]
        blocks = [
            jnp.where(head_of_row == h, main_values, jnp.zeros_like(main_values)) for h in range(4)
        ]
        blocks.append(jnp.where(tail_head == tail_row, tail_values, jnp.zeros_like(tail_values)))
        values = jnp.concatenate([jnp.concatenate(blocks, 1), sum_rows], 0)
        result = dot(values, weights)
        scale = 1.0 / result[128:136]
        return [result[32 * h : 32 * h + 32] * scale[h : h + 1] for h in range(4)]

    def attend_chunk():
        groups = HEADS // 4
        count = GROUP * groups
        parts, scores, weights, outs = {}, {}, {}, {i: [] for i in range(GROUP)}
        for t in range(count + 2):
            if t < count:
                i, g = divmod(t, groups)
                if g == 0:
                    parts[i] = window_parts(i)
                scores[t] = scores_of(i, g, parts[i])
            if 0 <= t - 2 < count:
                i, g = divmod(t - 2, groups)
                outs[i] += outs_of(g, parts[i], weights.pop(t - 2))
                if g == groups - 1:
                    out_t = jnp.concatenate(outs.pop(i), 0).astype(BF16)
                    wos[pl.ds(i * PADDED, PADDED)] = dot_nt(order[...], out_t).astype(BF16)
            if 0 <= t - 1 < count:
                weights[t - 1] = weights_of(scores.pop(t - 1))

    def merge(blocks):
        total = sum(jnp.sum(b, -1, keepdims=True) for b in blocks)
        mean = total * (1.0 / 2048)
        blocks = [b - mean for b in blocks]
        spread = sum(jnp.sum(b * b, -1, keepdims=True) for b in blocks) * (1.0 / 2048)
        factor = lax.rsqrt(spread + 1e-05)
        merge_in = jnp.concatenate([(b * factor).astype(BF16) for b in blocks], 1)
        return dot(merge_in, w_merge[...])

    def packed(rows40):
        stacked_lanes = jnp.concatenate([rows40[:, 512 * j : 512 * j + 512] for j in range(2)], 0)
        return dot(pack[...], stacked_lanes.astype(BF16)).astype(BF16)

    def own_copy():
        return pltpu.make_async_copy(
            stage.at[pl.ds(3 * lon, 3)], recv.at[lon], out_recv
        )

    def send_copy(owner):
        return pltpu.make_async_remote_copy(
            src_ref=stage.at[pl.ds(3 * owner, 3)],
            dst_ref=recv.at[lon],
            send_sem=out_send.at[owner],
            recv_sem=out_recv,
            device_id=(lat, owner),
            device_id_type=MESH,
        )

    def own_part(place, target, count):
        return pltpu.make_async_copy(
            stage.at[pl.ds(place, count)], recv.at[lon, pl.ds(target, count)], out_recv
        )

    def send_part(owner, place, target, count, sem):
        return remote(
            stage.at[pl.ds(place, count)],
            recv.at[lon, pl.ds(target, count)],
            out_send.at[sem],
            out_recv,
            (lat, owner),
        )

    def part_of(owner, place, target, count, sem):
        @pl.when(owner == lon)
        def _():
            own_part(place, target, count).start()

        @pl.when(owner != lon)
        def _():
            send_part(owner, place, target, count, sem).start()

    def last_copy():
        return pltpu.make_async_remote_copy(
            src_ref=stage.at[pl.ds(3 * windows, 1)],
            dst_ref=recv.at[lon, pl.ds(0, 1)],
            send_sem=out_send.at[windows],
            recv_sem=out_recv,
            device_id=(next_lat, 0),
            device_id_type=MESH,
        )

    def send(owner):
        @pl.when(owner == lon)
        def _():
            own_copy().start()

        @pl.when(owner != lon)
        def _():
            send_copy(owner).start()

    carry_copy = pltpu.make_async_remote_copy(
        src_ref=carry_send,
        dst_ref=carry_recv,
        send_sem=carry_sems.at[0],
        recv_sem=carry_sems.at[1],
        device_id=(next_lat, lon),
        device_id_type=MESH,
    )

    carry[...] = jnp.zeros_like(carry)
    slot_row = lax.broadcasted_iota(jnp.int32, (GROUP * 40, 512), 0) % 40 < 12

    def chunk_step(step, _):
        chunk = lax.rem(first + step, chunks)
        start = chunk * GROUP

        halo_case(chunk, first, lambda copy: copy.wait_recv())

        @pl.when(chunk == chunks - 1)
        def _():
            ahead[3].wait_recv()
            ahead[4].wait_recv()

        for i in range(GROUP):
            part = pl.ds(3 * chunk + PICK_STARTS[i], 2)
            raw = [
                jnp.concatenate(
                    [value[:, :, part].reshape(BLOCK, channels), marks[:, :, part].reshape(BLOCK, 128)],
                    1,
                )
                for value, marks in ((own, own_marks), (east, east_marks))
            ]
            value = dot(pick[i], jnp.concatenate(raw, 0))
            ms[pl.ds(i * SPAN, SPAN)] = value[:, channels:].astype(BF16)
            value = value[:, :channels]
            xs[pl.ds(i * SPAN, SPAN)] = value.astype(BF16)
            ns[pl.ds(i * SPAN, SPAN)] = normalize(value).astype(BF16)
        qs[...] = (dot(ns[...], w_qk[:, :512]) * score_scale).astype(BF16)
        ks[...] = dot(ns[...], w_qk[:, 512:]).astype(BF16)
        attend_chunk()
        residual = jnp.concatenate(
            [dot(order[...], xs[pl.ds(i * SPAN, SPAN)]) for i in range(GROUP)], 0
        )
        updated = (residual + dot(wos[...], w_out[...])).astype(BF16).astype(F32)
        blocks = []
        for p in range(4):
            pieces = [
                updated[PADDED * i + 40 * p : PADDED * i + 40 * p + 40] for i in range(GROUP)
            ]
            block = jnp.concatenate(pieces, 0)
            if p < 2:
                before = jnp.concatenate([carry[pl.ds(40 * p, 40)]] + pieces[:-1], 0)
                carry[pl.ds(40 * p, 40)] = pieces[-1]
                block = jnp.where(slot_row, before, block)
            blocks.append(block)

        @pl.when(step == 0)
        def _():
            for p in range(2):
                odd_save[1, pl.ds(16 * p, 16)] = blocks[2 + p][:16]

        @pl.when(chunk == 0)
        def _():
            for p in range(2):
                odd_save[0, pl.ds(16 * p, 16)] = blocks[2 + p][:16]

        @pl.when(chunk == chunks - 1)
        def _():
            for p in range(2):
                carry_send[pl.ds(16 * p, 16)] = carry[pl.ds(40 * p, 16)].astype(BF16)
            carry_copy.start()

        merged = merge(blocks)
        for i in range(GROUP):
            pieces = packed(merged[40 * i : 40 * i + 40])
            for slot in range(3):
                stage[3 * (start + i) + 1 + slot] = pieces[24 * slot : 24 * slot + 24].reshape(3, 8, 512)
            owner = start + i
            if i == 0:

                @pl.when(jnp.logical_and(step > 0, chunk > 0))
                def _():
                    send(owner)

                @pl.when(chunk == 0)
                def _():
                    part_of(0, 2, 2, 1, 0)

                @pl.when(jnp.logical_and(step == 0, chunk > 0))
                def _():
                    part_of(owner, 3 * owner + 2, 2, 1, owner)
            else:
                send(owner)

        @pl.when(chunk == chunks - 1)
        def _():
            last_copy().start()

        return 0

    lax.fori_loop(0, chunks, chunk_step, 0)

    carry_copy.wait_recv()
    lat_carry = carry_recv[...].astype(F32)
    rows_of = lambda p: pl.ds(16 * p, 16)
    pieces = [
        jnp.concatenate([lat_carry[16 * p : 16 * p + 16], carry[pl.ds(40 * p, 16)]], 0)
        for p in range(2)
    ]
    pieces += [jnp.concatenate([odd_save[0, rows_of(p)], odd_save[1, rows_of(p)]], 0) for p in range(2)]
    merged = merge(pieces)
    zero_rows = jnp.zeros((24, 2 * channels), F32)
    stage[1] = packed(jnp.concatenate([merged[:16], zero_rows], 0))[:24].reshape(3, 8, 512)
    part_of(0, 1, 1, 1, windows + 1)
    split = GROUP * first

    @pl.when(first != 0)
    def _():
        stage[3 * split + 1] = packed(jnp.concatenate([merged[16:], zero_rows], 0))[:24].reshape(3, 8, 512)
        part_of(split, 3 * split, 0, 2, windows + 2)

    def wait_halo(chunk, _):
        halo_case(chunk, first_west, lambda copy: copy.wait_send())
        return 0

    lax.fori_loop(0, chunks, wait_halo, 0)
    for copy in ahead:
        copy.wait_send()
    carry_copy.wait_send()
    last_copy().wait_send()

    @pl.when(lon != 0)
    def _():
        send_part(0, 2, 2, 1, 0).wait_send()
        send_part(0, 1, 1, 1, windows + 1).wait_send()

    @pl.when(jnp.logical_and(first != 0, split != lon))
    def _():
        send_part(split, 3 * split + 2, 2, 1, split).wait_send()
        send_part(split, 3 * split, 0, 2, windows + 2).wait_send()

    def wait_send(owner, _):
        @pl.when(jnp.logical_and(owner != lon, owner != split))
        def _():
            send_copy(owner).wait_send()

        return 0

    lax.fori_loop(1, windows, wait_send, 0)
    pltpu.make_async_copy(recv, recv, out_recv).wait()


def exchange(tokens, region, w_qkv, w_out, w_merge, n_lat, n_lon):
    levels, cols, tiles, _, channels = tokens.shape
    rows = tiles * 8
    windows = rows // WIN_LAT
    vmem = pl.BlockSpec(memory_space=pltpu.VMEM)
    hbm = pl.BlockSpec(memory_space=pl.ANY)
    span = GROUP * SPAN
    half = cols // 2
    return pl.pallas_call(
        functools.partial(fused, n_lat, n_lon),
        out_shape=jax.ShapeDtypeStruct((n_lon, 3, 3, 8, 512), BF16),
        in_specs=[hbm] * 2 + [vmem] * 3 + [hbm] * 3,
        out_specs=hbm,
        scratch_shapes=[
            pltpu.VMEM((levels, half, tiles + 1, 8, channels), BF16),
            pltpu.VMEM((levels, half, tiles + 1, 8, channels), BF16),
            pltpu.VMEM((half, levels, rows), jnp.int32),
            pltpu.VMEM((half, levels, rows), jnp.int32),
            pltpu.VMEM((half, levels, 128), jnp.int32),
            pltpu.VMEM((half, levels, 128), jnp.int32),
            pltpu.VMEM((levels, half, tiles + 1, 8, 128), BF16),
            pltpu.VMEM((levels, half, tiles + 1, 8, 128), BF16),
            pltpu.VMEM((3 * windows + 1, 3, 8, 512), BF16),
            pltpu.VMEM((channels, 2 * channels), BF16),
            pltpu.VMEM((channels, channels), BF16),
            pltpu.VMEM((channels, channels), BF16),
            pltpu.VMEM((channels, channels), BF16),
            pltpu.VMEM((4 * channels, 2 * channels), BF16),
            pltpu.VMEM((span, channels), BF16),
            pltpu.VMEM((span, channels), BF16),
            pltpu.VMEM((span, 128), BF16),
            pltpu.VMEM((span, channels), BF16),
            pltpu.VMEM((span, channels), BF16),
            pltpu.VMEM((GROUP * PADDED, channels), BF16),
            pltpu.VMEM((80, channels), F32),
            pltpu.VMEM((2, 32, channels), F32),
            pltpu.VMEM((32, channels), BF16),
            pltpu.VMEM((32, channels), BF16),
            pltpu.SemaphoreType.DMA((6,)),
            pltpu.SemaphoreType.DMA((5,)),
            pltpu.SemaphoreType.DMA((5,)),
            pltpu.SemaphoreType.DMA((windows // GROUP,)),
            pltpu.SemaphoreType.DMA((windows // GROUP,)),
            pltpu.SemaphoreType.DMA((2,)),
            pltpu.SemaphoreType.DMA((windows + 3,)),
            pltpu.SemaphoreType.DMA,
        ],
        compiler_params=pltpu.CompilerParams(
            collective_id=0, has_side_effects=True, vmem_limit_bytes=56 * 1024 * 1024
        ),
        name="attend_merge_send",
    )(tokens, region, *tables(), w_qkv, w_out, w_merge)


def place(table, pieces, out):
    sources = pieces.shape[0]
    for group in range(sources // 8):
        before = pieces[(8 * group + sources - 1) % sources, 0].reshape(24, 512)
        here = pieces[8 * group : 8 * group + 8, 0].reshape(192, 512)
        columns = dot(table[...], jnp.concatenate([before, here], 0)).astype(BF16)
        for lev in range(LEV):
            for lanes in range(2):
                at = (lev * 2 + lanes) * 48
                out[lev, 0, 48 * group : 48 * group + 48, 512 * lanes : 512 * lanes + 512] = (
                    columns[at : at + 48]
                )


def arrange(recv):
    n_lon = recv.shape[0]
    return pl.pallas_call(
        place,
        grid=(3,),
        out_shape=jax.ShapeDtypeStruct((LEV, 3, n_lon * 6, 1024), BF16),
        in_specs=[
            pl.BlockSpec((192, 216), lambda row: (0, 0)),
            pl.BlockSpec((n_lon, 1, 3, 8, 512), lambda row: (0, row, 0, 0, 0)),
        ],
        out_specs=pl.BlockSpec((LEV, 1, n_lon * 6, 1024), lambda row: (0, row, 0, 0)),
        name="place_columns",
    )(arrange_table(), recv)


def solution(mesh):
    n_lat, n_lon = mesh.shape["lat"], mesh.shape["lon"]

    def body(tokens, region, w_qkv, w_out, w_merge):
        levels, rows, cols, channels = tokens.shape
        by_column = tokens.transpose(0, 2, 1, 3).reshape(levels, cols, rows // 8, 8, channels)
        recv = exchange(
            by_column, region.transpose(2, 0, 1), w_qkv, w_out, w_merge, n_lat, n_lon
        )
        return arrange(recv)

    in_specs = (P(None, "lat", "lon", None), P(None, "lat", "lon"), P(), P(), P())
    out_specs = P(None, ("lat", "lon"), None, None)
    return jax.shard_map(body, mesh=mesh, in_specs=in_specs, out_specs=out_specs, check_vma=False)
```

```python
import functools

import jax
import jax.numpy as jnp
import numpy as np
from jax import lax
from jax.experimental import pallas as pl
from jax.experimental.pallas import tpu as pltpu
from jax.sharding import PartitionSpec as P

MESH = pl.DeviceIdType.MESH
HEADS = 16
WIN_LAT = 6
WIN_LON = 12
LEV = 2
BLOCK = 192
SPAN = 144
PADDED = 160
GROUP = 4
PICK_STARTS = (0, 1, 1, 2)
PICK_ROWS = (3, 1, 7, 5)
F32 = jnp.float32
BF16 = jnp.bfloat16


def tables():
    pick = np.zeros((SPAN, 2 * BLOCK), np.float32)
    order = np.zeros((PADDED, SPAN), np.float32)
    pack = np.zeros((SPAN // 2, PADDED // 2), np.float32)
    picks = []
    for offset in PICK_ROWS:
        pick = np.zeros((SPAN, 2 * BLOCK), np.float32)
        for line in range(24):
            for row in range(6):
                pick[line * 6 + row, line * 16 + offset + row] = 1
        picks.append(pick)
    window_rows = ((5, 1, 3), (0, 2, 4))
    for odd in range(2):
        for right in range(2):
            block = odd * 2 + right
            for slot in range(3):
                for lev in range(LEV):
                    for patch in range(6):
                        half, col = divmod(patch, 3)
                        line = half * 12 + lev * 6 + 2 * col + right
                        token = line * 6 + window_rows[odd][slot]
                        order[block * 40 + slot * 12 + lev * 6 + patch, token] = 1
    for slot in range(3):
        for lanes in range(2):
            for place in range(12):
                pack[slot * 24 + lanes * 12 + place, lanes * 40 + slot * 12 + place] = 1
    return [jnp.asarray(t, BF16) for t in (np.stack(picks), order, pack)]


def arrange_table():
    table = np.zeros((192, 216), np.float32)
    for lev in range(LEV):
        for lanes in range(2):
            for col in range(48):
                device, place = divmod(col, 6)
                source, patch = (device, 3 + place) if place < 3 else (device + 1, place - 3)
                piece = source * 24 + lanes * 12 + lev * 6 + patch
                table[(lev * 2 + lanes) * 48 + col, piece] = 1
    return jnp.asarray(table, BF16)


def dot(a, b):
    return jnp.dot(a, b, preferred_element_type=F32)


def dot_nt(a, b):
    return lax.dot_general(a, b, (((1,), (1,)), ((), ())), preferred_element_type=F32)


def normalize(values):
    center = values - jnp.mean(values, -1, keepdims=True)
    spread = jnp.mean(center * center, -1, keepdims=True)
    return center * lax.rsqrt(spread + 1e-05)


def fused(
    n_lat,
    n_lon,
    tokens,
    region,
    pick,
    order,
    pack,
    w_qkv_hbm,
    w_out_hbm,
    w_merge_hbm,
    recv,
    own,
    east,
    own_region,
    east_region,
    own_next,
    east_next,
    own_marks,
    east_marks,
    stage,
    w_qk,
    w_v,
    w_vt,
    w_out,
    w_merge,
    xs,
    ns,
    ms,
    qs,
    ks,
    wos,
    carry,
    odd_save,
    carry_send,
    carry_recv,
    top_rows,
    top_send,
    top_recv,
    load_sems,
    row_send,
    row_recv,
    halo_send,
    halo_recv,
    carry_sems,
    out_send,
    out_recv,
):
    lat = lax.axis_index("lat")
    lon = lax.axis_index("lon")
    next_lat = lax.rem(lat + 1, n_lat)
    prev_lat = lax.rem(lat + n_lat - 1, n_lat)
    west_lon = lax.rem(lon + n_lon - 1, n_lon)
    east_lon = lax.rem(lon + 1, n_lon)
    rows = tokens.shape[2] * 8
    channels = tokens.shape[4]
    windows = rows // WIN_LAT
    chunks = windows // GROUP

    def first_chunk(place):
        return place // 4

    first = first_chunk(lon)
    first_west = first_chunk(west_lon)

    loads = [
        pltpu.make_async_copy(tokens.at[:, 6:12], own.at[:, :, : rows // 8], load_sems.at[0]),
        pltpu.make_async_copy(region.at[6:12], own_region, load_sems.at[1]),
        pltpu.make_async_copy(w_qkv_hbm.at[:, : 2 * channels], w_qk, load_sems.at[2]),
        pltpu.make_async_copy(w_qkv_hbm.at[:, 2 * channels :], w_v, load_sems.at[3]),
        pltpu.make_async_copy(w_out_hbm, w_out, load_sems.at[4]),
        pltpu.make_async_copy(w_merge_hbm, w_merge, load_sems.at[5]),
        pltpu.make_async_copy(tokens.at[:, :, 0:1], top_rows, load_sems.at[6]),
    ]
    for load in loads:
        load.start()

    barrier = pltpu.get_barrier_semaphore()

    def greet(step, _):
        other = lax.rem(lon + step, n_lon)
        pl.semaphore_signal(barrier, inc=1, device_id=(lat, other), device_id_type=MESH)
        return 0

    lax.fori_loop(1, n_lon, greet, 0)
    pl.semaphore_signal(barrier, inc=1, device_id=(prev_lat, lon), device_id_type=MESH)
    pl.semaphore_signal(barrier, inc=1, device_id=(next_lat, lon), device_id_type=MESH)
    pl.semaphore_signal(barrier, inc=1, device_id=(next_lat, east_lon), device_id_type=MESH)

    @pl.when(lon == 0)
    def _():
        def greet_before(other, _):
            pl.semaphore_signal(barrier, inc=1, device_id=(prev_lat, other), device_id_type=MESH)
            return 0

        lax.fori_loop(0, n_lon, greet_before, 0)

    pl.semaphore_wait(barrier, n_lon + 3)

    def remote(source, target, send_sem, recv_sem, device):
        return pltpu.make_async_remote_copy(
            src_ref=source,
            dst_ref=target,
            send_sem=send_sem,
            recv_sem=recv_sem,
            device_id=device,
            device_id_type=MESH,
        )

    def halo_copy(chunk, start, count):
        part = pl.ds(start, count)
        return remote(
            tokens.at[:, 0:6, part],
            east.at[:, :, part],
            halo_send.at[chunk],
            halo_recv.at[chunk],
            (lat, west_lon),
        )

    def halo_case(chunk, start_chunk, act):
        head = jnp.logical_or(chunk == start_chunk, chunk == 0)
        short = jnp.logical_or(chunk == chunks - 1, chunk + 1 == start_chunk)
        for is_head in (False, True):
            for is_short in (False, True):

                @pl.when(jnp.logical_and(head == is_head, short == is_short))
                def _():
                    count = 3 + int(is_head) - int(is_short)
                    act(halo_copy(chunk, 3 * chunk + 1 - int(is_head), count))

    def send_west(step, _):
        halo_case(lax.rem(first_west + step, chunks), first_west, lambda copy: copy.start())
        return 0

    line = lax.broadcasted_iota(jnp.int32, (40, 96), 0)
    spot = lax.broadcasted_iota(jnp.int32, (40, 96), 1)
    gather_top = (line // 3 * 8 + line % 3 == spot).astype(F32).astype(BF16)
    spot = lax.broadcasted_iota(jnp.int32, (96, 40), 0)
    line = lax.broadcasted_iota(jnp.int32, (96, 40), 1)
    spread_top = (line // 3 * 8 + line % 3 == spot).astype(F32).astype(BF16)
    ahead = [
        remote(region.at[0:6], east_region, row_send.at[0], row_recv.at[0], (lat, west_lon)),
        remote(
            region.at[6:12, :, :128], own_next, row_send.at[1], row_recv.at[1], (prev_lat, lon)
        ),
        remote(
            region.at[0:6, :, :128],
            east_next,
            row_send.at[2],
            row_recv.at[2],
            (prev_lat, west_lon),
        ),
        remote(
            top_send.at[0],
            top_recv.at[0],
            row_send.at[3],
            row_recv.at[3],
            (prev_lat, lon),
        ),
        remote(
            top_send.at[1],
            top_recv.at[1],
            row_send.at[4],
            row_recv.at[4],
            (prev_lat, west_lon),
        ),
    ]
    for copy in ahead[:3]:
        copy.start()
    lax.fori_loop(0, 1, send_west, 0)
    loads[6].wait()
    for half in range(2):
        top = top_rows[:, 6 - 6 * half : 12 - 6 * half].reshape(96, channels)
        top_send[half] = dot(gather_top, top).astype(BF16).reshape(5, 8, channels)
        ahead[3 + half].start()
    lax.fori_loop(1, chunks, send_west, 0)

    def eye(size):
        row = lax.broadcasted_iota(jnp.int32, (size, size), 0)
        return (row == lax.broadcasted_iota(jnp.int32, (size, size), 1)).astype(F32).astype(BF16)

    def one_hot(lane_labels):
        label = lax.broadcasted_iota(jnp.int32, (128, lane_labels.shape[1]), 0)
        return (label == lane_labels).astype(F32).astype(BF16)

    pole = (lat == n_lat - 1).astype(jnp.int32)
    row_eye = eye(rows)
    next_eye = eye(128)[:8]

    def mark_half(here, after, marks):
        def mark_column(col, _):
            for lev in range(LEV):
                labels = here[col, lev : lev + 1] * 2
                marks[lev, col, pl.ds(0, rows // 8)] = (
                    dot_nt(row_eye, one_hot(labels)).astype(BF16).reshape(rows // 8, 8, 128)
                )
                labels = after[col, lev : lev + 1] * 2 + pole
                marks[lev, col, rows // 8] = dot_nt(next_eye, one_hot(labels)).astype(BF16)
            return 0

        lax.fori_loop(0, 6, mark_column, 0)

    loads[1].wait()
    ahead[1].wait_recv()
    mark_half(own_region, own_next, own_marks)
    loads[3].wait()
    w_vt[...] = dot_nt(eye(channels), w_v[...]).astype(BF16)
    ahead[0].wait_recv()
    ahead[2].wait_recv()
    mark_half(east_region, east_next, east_marks)
    for load in (loads[0], loads[2], loads[4], loads[5]):
        load.wait()

    score_scale = 32 ** (-0.5) * 1.4426950408889634
    head_of_lane = lax.broadcasted_iota(jnp.int32, (SPAN, 128), 1) // 32
    head_of_row = lax.broadcasted_iota(jnp.int32, (128, 128), 0) // 32
    tail_head = lax.broadcasted_iota(jnp.int32, (128, 64), 1) // 16
    tail_row = lax.broadcasted_iota(jnp.int32, (128, 64), 0) // 32
    sum_row = lax.broadcasted_iota(jnp.int32, (16, 512), 0)
    sum_lane = lax.broadcasted_iota(jnp.int32, (16, 512), 1) // 128
    tail_sum_row = lax.broadcasted_iota(jnp.int32, (16, 64), 0)
    tail_sum_lane = lax.broadcasted_iota(jnp.int32, (16, 64), 1) // 16
    sum_rows = jnp.concatenate(
        [(sum_row == sum_lane).astype(F32), (tail_sum_row == tail_sum_lane).astype(F32)], 1
    ).astype(BF16)
    def stacked(value):
        return jnp.concatenate([value[:128]] * 4 + [value[128:]] * 4, 0)

    def window_parts(i):
        normed = ns[pl.ds(i * SPAN, SPAN)]
        value_t = dot_nt(
            w_vt[...], jnp.concatenate([normed[:128]] + [normed[128:]] * 4, 0)
        ).astype(BF16)
        marks = ms[pl.ds(i * SPAN, SPAN)]
        key_marks = stacked(((marks.astype(F32) - 1.0) * 1e30).astype(BF16))
        return value_t, marks, key_marks

    def scores_of(i, g, parts):
        base = i * SPAN
        lanes = pl.ds(g * 128, 128)
        query = jnp.concatenate([qs[pl.ds(base, SPAN), lanes], parts[1]], 1)
        key = ks[pl.ds(base, SPAN), lanes]
        heads = [jnp.where(head_of_lane == h, key, jnp.zeros_like(key)) for h in range(4)]
        keys = jnp.concatenate([k[:128] for k in heads] + [k[128:] for k in heads], 0)
        return dot_nt(jnp.concatenate([keys, parts[2]], 1), query)

    def weights_of(scores):
        mains, tails = [], []
        for h in range(4):
            main = scores[128 * h : 128 * h + 128]
            tail = scores[512 + 16 * h : 528 + 16 * h]
            peak = jnp.maximum(jnp.max(main, 0, keepdims=True), jnp.max(tail, 0, keepdims=True))
            mains.append(jnp.exp2((main - peak).astype(BF16)))
            tails.append(jnp.exp2((tail - peak).astype(BF16)))
        return jnp.concatenate(mains + tails, 0)

    def outs_of(g, parts, weights):
        group_values = parts[0][g * 128 : g * 128 + 128]
        main_values = group_values[:, :128]
        tail_values = group_values[:, 128:192]
        blocks = [
            jnp.where(head_of_row == h, main_values, jnp.zeros_like(main_values)) for h in range(4)
        ]
        blocks.append(jnp.where(tail_head == tail_row, tail_values, jnp.zeros_like(tail_values)))
        values = jnp.concatenate([jnp.concatenate(blocks, 1), sum_rows], 0)
        result = dot(values, weights)
        scale = 1.0 / result[128:136]
        return [result[32 * h : 32 * h + 32] * scale[h : h + 1] for h in range(4)]

    def attend_chunk():
        groups = HEADS // 4
        count = GROUP * groups
        parts, scores, weights, outs = {}, {}, {}, {i: [] for i in range(GROUP)}
        for t in range(count + 2):
            if t < count:
                i, g = divmod(t, groups)
                if g == 0:
                    parts[i] = window_parts(i)
                scores[t] = scores_of(i, g, parts[i])
            if 0 <= t - 2 < count:
                i, g = divmod(t - 2, groups)
                outs[i] += outs_of(g, parts[i], weights.pop(t - 2))
                if g == groups - 1:
                    out_t = jnp.concatenate(outs.pop(i), 0).astype(BF16)
                    wos[pl.ds(i * PADDED, PADDED)] = dot_nt(order[...], out_t).astype(BF16)
            if 0 <= t - 1 < count:
                weights[t - 1] = weights_of(scores.pop(t - 1))

    def merge(blocks):
        total = sum(jnp.sum(b, -1, keepdims=True) for b in blocks)
        mean = total * (1.0 / 2048)
        blocks = [b - mean for b in blocks]
        spread = sum(jnp.sum(b * b, -1, keepdims=True) for b in blocks) * (1.0 / 2048)
        factor = lax.rsqrt(spread + 1e-05)
        merge_in = jnp.concatenate([(b * factor).astype(BF16) for b in blocks], 1)
        return dot(merge_in, w_merge[...])

    def packed(rows40):
        stacked_lanes = jnp.concatenate([rows40[:, 512 * j : 512 * j + 512] for j in range(2)], 0)
        return dot(pack[...], stacked_lanes.astype(BF16)).astype(BF16)

    def own_copy():
        return pltpu.make_async_copy(
            stage.at[pl.ds(3 * lon, 3)], recv.at[lon], out_recv
        )

    def send_copy(owner):
        return pltpu.make_async_remote_copy(
            src_ref=stage.at[pl.ds(3 * owner, 3)],
            dst_ref=recv.at[lon],
            send_sem=out_send.at[owner],
            recv_sem=out_recv,
            device_id=(lat, owner),
            device_id_type=MESH,
        )

    def own_part(place, target, count):
        return pltpu.make_async_copy(
            stage.at[pl.ds(place, count)], recv.at[lon, pl.ds(target, count)], out_recv
        )

    def send_part(owner, place, target, count, sem):
        return remote(
            stage.at[pl.ds(place, count)],
            recv.at[lon, pl.ds(target, count)],
            out_send.at[sem],
            out_recv,
            (lat, owner),
        )

    def part_of(owner, place, target, count, sem):
        @pl.when(owner == lon)
        def _():
            own_part(place, target, count).start()

        @pl.when(owner != lon)
        def _():
            send_part(owner, place, target, count, sem).start()

    def last_copy():
        return pltpu.make_async_remote_copy(
            src_ref=stage.at[pl.ds(3 * windows, 1)],
            dst_ref=recv.at[lon, pl.ds(0, 1)],
            send_sem=out_send.at[windows],
            recv_sem=out_recv,
            device_id=(next_lat, 0),
            device_id_type=MESH,
        )

    def send(owner):
        @pl.when(owner == lon)
        def _():
            own_copy().start()

        @pl.when(owner != lon)
        def _():
            send_copy(owner).start()

    carry_copy = pltpu.make_async_remote_copy(
        src_ref=carry_send,
        dst_ref=carry_recv,
        send_sem=carry_sems.at[0],
        recv_sem=carry_sems.at[1],
        device_id=(next_lat, lon),
        device_id_type=MESH,
    )

    def finish_first(before, saved, place):
        pieces = [before[16 * p : 16 * p + 16] for p in range(2)]
        pieces += [odd_save[saved, pl.ds(16 * p, 16)] for p in range(2)]
        merged = jnp.concatenate([merge(pieces), jnp.zeros((24, 2 * channels), F32)], 0)
        stage[place] = packed(merged)[:24].reshape(3, 8, 512)

    carry[...] = jnp.zeros_like(carry)
    slot_row = lax.broadcasted_iota(jnp.int32, (GROUP * 40, 512), 0) % 40 < 12

    def chunk_step(step, _):
        chunk = lax.rem(first + step, chunks)
        start = chunk * GROUP

        halo_case(chunk, first, lambda copy: copy.wait_recv())

        @pl.when(chunk == chunks - 1)
        def _():
            for half, target in enumerate((own, east)):
                ahead[3 + half].wait_recv()
                top = dot(spread_top, top_recv[half].reshape(40, channels)).astype(BF16)
                target[:, :, rows // 8] = top.reshape(LEV, 6, 8, channels)

        for i in range(GROUP):
            part = pl.ds(3 * chunk + PICK_STARTS[i], 2)
            raw = [
                jnp.concatenate(
                    [value[:, :, part].reshape(BLOCK, channels), marks[:, :, part].reshape(BLOCK, 128)],
                    1,
                )
                for value, marks in ((own, own_marks), (east, east_marks))
            ]
            value = dot(pick[i], jnp.concatenate(raw, 0))
            ms[pl.ds(i * SPAN, SPAN)] = value[:, channels:].astype(BF16)
            value = value[:, :channels]
            xs[pl.ds(i * SPAN, SPAN)] = value.astype(BF16)
            ns[pl.ds(i * SPAN, SPAN)] = normalize(value).astype(BF16)
        qs[...] = (dot(ns[...], w_qk[:, :512]) * score_scale).astype(BF16)
        ks[...] = dot(ns[...], w_qk[:, 512:]).astype(BF16)
        attend_chunk()
        residual = jnp.concatenate(
            [dot(order[...], xs[pl.ds(i * SPAN, SPAN)]) for i in range(GROUP)], 0
        )
        updated = (residual + dot(wos[...], w_out[...])).astype(BF16).astype(F32)
        blocks = []
        for p in range(4):
            pieces = [
                updated[PADDED * i + 40 * p : PADDED * i + 40 * p + 40] for i in range(GROUP)
            ]
            block = jnp.concatenate(pieces, 0)
            if p < 2:
                before = jnp.concatenate([carry[pl.ds(40 * p, 40)]] + pieces[:-1], 0)
                carry[pl.ds(40 * p, 40)] = pieces[-1]
                block = jnp.where(slot_row, before, block)
            blocks.append(block)

        @pl.when(step == 0)
        def _():
            for p in range(2):
                odd_save[1, pl.ds(16 * p, 16)] = blocks[2 + p][:16]

        @pl.when(chunk == 0)
        def _():
            for p in range(2):
                odd_save[0, pl.ds(16 * p, 16)] = blocks[2 + p][:16]

        @pl.when(chunk == chunks - 1)
        def _():
            for p in range(2):
                carry_send[pl.ds(16 * p, 16)] = carry[pl.ds(40 * p, 16)].astype(BF16)
            carry_copy.start()

        merged = merge(blocks)
        for i in range(GROUP):
            pieces = packed(merged[40 * i : 40 * i + 40])
            for slot in range(3):
                stage[3 * (start + i) + 1 + slot] = pieces[24 * slot : 24 * slot + 24].reshape(3, 8, 512)
            owner = start + i
            if i == 0:

                @pl.when(jnp.logical_and(step > 0, chunk > 0))
                def _():
                    send(owner)

                @pl.when(chunk == 0)
                def _():
                    part_of(0, 2, 2, 1, 0)

                @pl.when(jnp.logical_and(step == 0, chunk > 0))
                def _():
                    part_of(owner, 3 * owner + 2, 2, 1, owner)
            else:
                send(owner)

        @pl.when(chunk == chunks - 1)
        def _():
            last_copy().start()

        @pl.when(jnp.logical_and(step == chunks - 1, first != 0))
        def _():
            carry_copy.wait_recv()
            finish_first(carry_recv[...].astype(F32), 0, 1)
            part_of(0, 1, 1, 1, windows + 1)

        return 0

    lax.fori_loop(0, chunks, chunk_step, 0)

    @pl.when(first == 0)
    def _():
        carry_copy.wait_recv()
        finish_first(carry_recv[...].astype(F32), 0, 1)
        part_of(0, 1, 1, 1, windows + 1)

    split = GROUP * first

    @pl.when(first != 0)
    def _():
        last = jnp.concatenate([carry[pl.ds(40 * p, 16)] for p in range(2)], 0)
        finish_first(last, 1, 3 * split + 1)
        part_of(split, 3 * split, 0, 2, windows + 2)

    def wait_halo(chunk, _):
        halo_case(chunk, first_west, lambda copy: copy.wait_send())
        return 0

    lax.fori_loop(0, chunks, wait_halo, 0)
    for copy in ahead:
        copy.wait_send()
    carry_copy.wait_send()
    last_copy().wait_send()

    @pl.when(lon != 0)
    def _():
        send_part(0, 2, 2, 1, 0).wait_send()
        send_part(0, 1, 1, 1, windows + 1).wait_send()

    @pl.when(jnp.logical_and(first != 0, split != lon))
    def _():
        send_part(split, 3 * split + 2, 2, 1, split).wait_send()
        send_part(split, 3 * split, 0, 2, windows + 2).wait_send()

    def wait_send(owner, _):
        @pl.when(jnp.logical_and(owner != lon, owner != split))
        def _():
            send_copy(owner).wait_send()

        return 0

    lax.fori_loop(1, windows, wait_send, 0)
    pltpu.make_async_copy(recv, recv, out_recv).wait()


def exchange(tokens, region, w_qkv, w_out, w_merge, n_lat, n_lon):
    levels, cols, tiles, _, channels = tokens.shape
    rows = tiles * 8
    windows = rows // WIN_LAT
    vmem = pl.BlockSpec(memory_space=pltpu.VMEM)
    hbm = pl.BlockSpec(memory_space=pl.ANY)
    span = GROUP * SPAN
    half = cols // 2
    return pl.pallas_call(
        functools.partial(fused, n_lat, n_lon),
        out_shape=jax.ShapeDtypeStruct((n_lon, 3, 3, 8, 512), BF16),
        in_specs=[hbm] * 2 + [vmem] * 3 + [hbm] * 3,
        out_specs=hbm,
        scratch_shapes=[
            pltpu.VMEM((levels, half, tiles + 1, 8, channels), BF16),
            pltpu.VMEM((levels, half, tiles + 1, 8, channels), BF16),
            pltpu.VMEM((half, levels, rows), jnp.int32),
            pltpu.VMEM((half, levels, rows), jnp.int32),
            pltpu.VMEM((half, levels, 128), jnp.int32),
            pltpu.VMEM((half, levels, 128), jnp.int32),
            pltpu.VMEM((levels, half, tiles + 1, 8, 128), BF16),
            pltpu.VMEM((levels, half, tiles + 1, 8, 128), BF16),
            pltpu.VMEM((3 * windows + 1, 3, 8, 512), BF16),
            pltpu.VMEM((channels, 2 * channels), BF16),
            pltpu.VMEM((channels, channels), BF16),
            pltpu.VMEM((channels, channels), BF16),
            pltpu.VMEM((channels, channels), BF16),
            pltpu.VMEM((4 * channels, 2 * channels), BF16),
            pltpu.VMEM((span, channels), BF16),
            pltpu.VMEM((span, channels), BF16),
            pltpu.VMEM((span, 128), BF16),
            pltpu.VMEM((span, channels), BF16),
            pltpu.VMEM((span, channels), BF16),
            pltpu.VMEM((GROUP * PADDED, channels), BF16),
            pltpu.VMEM((80, channels), F32),
            pltpu.VMEM((2, 32, channels), F32),
            pltpu.VMEM((32, channels), BF16),
            pltpu.VMEM((32, channels), BF16),
            pltpu.VMEM((levels, cols, 1, 8, channels), BF16),
            pltpu.VMEM((2, 5, 8, channels), BF16),
            pltpu.VMEM((2, 5, 8, channels), BF16),
            pltpu.SemaphoreType.DMA((7,)),
            pltpu.SemaphoreType.DMA((5,)),
            pltpu.SemaphoreType.DMA((5,)),
            pltpu.SemaphoreType.DMA((windows // GROUP,)),
            pltpu.SemaphoreType.DMA((windows // GROUP,)),
            pltpu.SemaphoreType.DMA((2,)),
            pltpu.SemaphoreType.DMA((windows + 3,)),
            pltpu.SemaphoreType.DMA,
        ],
        compiler_params=pltpu.CompilerParams(
            collective_id=0, has_side_effects=True, vmem_limit_bytes=56 * 1024 * 1024
        ),
        name="attend_merge_send",
    )(tokens, region, *tables(), w_qkv, w_out, w_merge)


def place(table, pieces, out):
    sources = pieces.shape[0]
    for group in range(sources // 8):
        before = pieces[(8 * group + sources - 1) % sources, 0].reshape(24, 512)
        here = pieces[8 * group : 8 * group + 8, 0].reshape(192, 512)
        columns = dot(table[...], jnp.concatenate([before, here], 0)).astype(BF16)
        for lev in range(LEV):
            for lanes in range(2):
                at = (lev * 2 + lanes) * 48
                out[lev, 0, 48 * group : 48 * group + 48, 512 * lanes : 512 * lanes + 512] = (
                    columns[at : at + 48]
                )


def arrange(recv):
    n_lon = recv.shape[0]
    return pl.pallas_call(
        place,
        grid=(3,),
        out_shape=jax.ShapeDtypeStruct((LEV, 3, n_lon * 6, 1024), BF16),
        in_specs=[
            pl.BlockSpec((192, 216), lambda row: (0, 0)),
            pl.BlockSpec((n_lon, 1, 3, 8, 512), lambda row: (0, row, 0, 0, 0)),
        ],
        out_specs=pl.BlockSpec((LEV, 1, n_lon * 6, 1024), lambda row: (0, row, 0, 0)),
        name="place_columns",
    )(arrange_table(), recv)


def solution(mesh):
    n_lat, n_lon = mesh.shape["lat"], mesh.shape["lon"]

    def body(tokens, region, w_qkv, w_out, w_merge):
        levels, rows, cols, channels = tokens.shape
        by_column = tokens.transpose(0, 2, 1, 3).reshape(levels, cols, rows // 8, 8, channels)
        recv = exchange(
            by_column, region.transpose(2, 0, 1), w_qkv, w_out, w_merge, n_lat, n_lon
        )
        return arrange(recv)

    in_specs = (P(None, "lat", "lon", None), P(None, "lat", "lon"), P(), P(), P())
    out_specs = P(None, ("lat", "lon"), None, None)
    return jax.shard_map(body, mesh=mesh, in_specs=in_specs, out_specs=out_specs, check_vma=False)
```

```python
import functools

import jax
import jax.numpy as jnp
import numpy as np
from jax import lax
from jax.experimental import pallas as pl
from jax.experimental.pallas import tpu as pltpu
from jax.sharding import PartitionSpec as P

MESH = pl.DeviceIdType.MESH
HEADS = 16
WIN_LAT = 6
WIN_LON = 12
LEV = 2
BLOCK = 192
SPAN = 144
PADDED = 160
GROUP = 4
PICK_STARTS = (0, 1, 1, 2)
PICK_ROWS = (3, 1, 7, 5)
F32 = jnp.float32
BF16 = jnp.bfloat16


def tables():
    pick = np.zeros((SPAN, 2 * BLOCK), np.float32)
    order = np.zeros((PADDED, SPAN), np.float32)
    pack = np.zeros((SPAN // 2, PADDED // 2), np.float32)
    picks = []
    for offset in PICK_ROWS:
        pick = np.zeros((SPAN, 2 * BLOCK), np.float32)
        for line in range(24):
            for row in range(6):
                pick[line * 6 + row, line * 16 + offset + row] = 1
        picks.append(pick)
    window_rows = ((5, 1, 3), (0, 2, 4))
    for odd in range(2):
        for right in range(2):
            block = odd * 2 + right
            for slot in range(3):
                for lev in range(LEV):
                    for patch in range(6):
                        half, col = divmod(patch, 3)
                        line = half * 12 + lev * 6 + 2 * col + right
                        token = line * 6 + window_rows[odd][slot]
                        order[block * 40 + slot * 12 + lev * 6 + patch, token] = 1
    for slot in range(3):
        for lanes in range(2):
            for place in range(12):
                pack[slot * 24 + lanes * 12 + place, lanes * 40 + slot * 12 + place] = 1
    return [jnp.asarray(t, BF16) for t in (np.stack(picks), order, pack)]


def arrange_table():
    table = np.zeros((192, 216), np.float32)
    for lev in range(LEV):
        for lanes in range(2):
            for col in range(48):
                device, place = divmod(col, 6)
                source, patch = (device, 3 + place) if place < 3 else (device + 1, place - 3)
                piece = source * 24 + lanes * 12 + lev * 6 + patch
                table[(lev * 2 + lanes) * 48 + col, piece] = 1
    return jnp.asarray(table, BF16)


def dot(a, b):
    return jnp.dot(a, b, preferred_element_type=F32)


def dot_nt(a, b):
    return lax.dot_general(a, b, (((1,), (1,)), ((), ())), preferred_element_type=F32)


def normalize(values):
    center = values - jnp.mean(values, -1, keepdims=True)
    spread = jnp.mean(center * center, -1, keepdims=True)
    return center * lax.rsqrt(spread + 1e-05)


def fused(
    n_lat,
    n_lon,
    tokens,
    region,
    pick,
    order,
    pack,
    w_qkv_hbm,
    w_out_hbm,
    w_merge_hbm,
    recv,
    own,
    east,
    own_region,
    east_region,
    own_next,
    east_next,
    own_marks,
    east_marks,
    stage,
    w_qk,
    w_v,
    w_vt,
    w_out,
    w_merge,
    xs,
    ns,
    ms,
    qs,
    ks,
    wos,
    carry,
    odd_save,
    carry_send,
    carry_recv,
    top_rows,
    top_send,
    top_recv,
    load_sems,
    row_send,
    row_recv,
    halo_send,
    halo_recv,
    carry_sems,
    out_send,
    out_recv,
):
    lat = lax.axis_index("lat")
    lon = lax.axis_index("lon")
    next_lat = lax.rem(lat + 1, n_lat)
    prev_lat = lax.rem(lat + n_lat - 1, n_lat)
    west_lon = lax.rem(lon + n_lon - 1, n_lon)
    east_lon = lax.rem(lon + 1, n_lon)
    rows = tokens.shape[2] * 8
    channels = tokens.shape[4]
    windows = rows // WIN_LAT
    chunks = windows // GROUP

    def first_chunk(place):
        return place // 4

    first = first_chunk(lon)
    first_west = first_chunk(west_lon)

    loads = [
        pltpu.make_async_copy(tokens.at[:, 6:12], own.at[:, :, : rows // 8], load_sems.at[0]),
        pltpu.make_async_copy(region.at[6:12], own_region, load_sems.at[1]),
        pltpu.make_async_copy(w_qkv_hbm.at[:, : 2 * channels], w_qk, load_sems.at[2]),
        pltpu.make_async_copy(w_qkv_hbm.at[:, 2 * channels :], w_v, load_sems.at[3]),
        pltpu.make_async_copy(w_out_hbm, w_out, load_sems.at[4]),
        pltpu.make_async_copy(w_merge_hbm, w_merge, load_sems.at[5]),
        pltpu.make_async_copy(tokens.at[:, :, 0:1], top_rows, load_sems.at[6]),
    ]
    barrier = pltpu.get_barrier_semaphore()

    def greet(step, _):
        other = lax.rem(lon + step, n_lon)
        pl.semaphore_signal(barrier, inc=1, device_id=(lat, other), device_id_type=MESH)
        return 0

    lax.fori_loop(1, n_lon, greet, 0)
    pl.semaphore_signal(barrier, inc=1, device_id=(prev_lat, lon), device_id_type=MESH)
    pl.semaphore_signal(barrier, inc=1, device_id=(next_lat, lon), device_id_type=MESH)
    pl.semaphore_signal(barrier, inc=1, device_id=(next_lat, east_lon), device_id_type=MESH)

    @pl.when(lon == 0)
    def _():
        def greet_before(other, _):
            pl.semaphore_signal(barrier, inc=1, device_id=(prev_lat, other), device_id_type=MESH)
            return 0

        lax.fori_loop(0, n_lon, greet_before, 0)

    for load in loads:
        load.start()

    pl.semaphore_wait(barrier, n_lon + 3)

    def remote(source, target, send_sem, recv_sem, device):
        return pltpu.make_async_remote_copy(
            src_ref=source,
            dst_ref=target,
            send_sem=send_sem,
            recv_sem=recv_sem,
            device_id=device,
            device_id_type=MESH,
        )

    def halo_copy(chunk, start, count):
        part = pl.ds(start, count)
        return remote(
            tokens.at[:, 0:6, part],
            east.at[:, :, part],
            halo_send.at[chunk],
            halo_recv.at[chunk],
            (lat, west_lon),
        )

    def halo_case(chunk, start_chunk, act):
        head = jnp.logical_or(chunk == start_chunk, chunk == 0)
        short = jnp.logical_or(chunk == chunks - 1, chunk + 1 == start_chunk)
        for is_head in (False, True):
            for is_short in (False, True):

                @pl.when(jnp.logical_and(head == is_head, short == is_short))
                def _():
                    count = 3 + int(is_head) - int(is_short)
                    act(halo_copy(chunk, 3 * chunk + 1 - int(is_head), count))

    def send_west(step, _):
        halo_case(lax.rem(first_west + step, chunks), first_west, lambda copy: copy.start())
        return 0

    line = lax.broadcasted_iota(jnp.int32, (40, 96), 0)
    spot = lax.broadcasted_iota(jnp.int32, (40, 96), 1)
    gather_top = (line // 3 * 8 + line % 3 == spot).astype(F32).astype(BF16)
    spot = lax.broadcasted_iota(jnp.int32, (96, 40), 0)
    line = lax.broadcasted_iota(jnp.int32, (96, 40), 1)
    spread_top = (line // 3 * 8 + line % 3 == spot).astype(F32).astype(BF16)
    ahead = [
        remote(region.at[0:6], east_region, row_send.at[0], row_recv.at[0], (lat, west_lon)),
        remote(
            region.at[6:12, :, :128], own_next, row_send.at[1], row_recv.at[1], (prev_lat, lon)
        ),
        remote(
            region.at[0:6, :, :128],
            east_next,
            row_send.at[2],
            row_recv.at[2],
            (prev_lat, west_lon),
        ),
        remote(
            top_send.at[0],
            top_recv.at[0],
            row_send.at[3],
            row_recv.at[3],
            (prev_lat, lon),
        ),
        remote(
            top_send.at[1],
            top_recv.at[1],
            row_send.at[4],
            row_recv.at[4],
            (prev_lat, west_lon),
        ),
    ]
    for copy in ahead[:3]:
        copy.start()
    lax.fori_loop(0, 1, send_west, 0)
    loads[6].wait()
    for half in range(2):
        top = top_rows[:, 6 - 6 * half : 12 - 6 * half].reshape(96, channels)
        top_send[half] = dot(gather_top, top).astype(BF16).reshape(5, 8, channels)
        ahead[3 + half].start()
    lax.fori_loop(1, chunks, send_west, 0)

    def eye(size):
        row = lax.broadcasted_iota(jnp.int32, (size, size), 0)
        return (row == lax.broadcasted_iota(jnp.int32, (size, size), 1)).astype(F32).astype(BF16)

    def one_hot(lane_labels):
        label = lax.broadcasted_iota(jnp.int32, (128, lane_labels.shape[1]), 0)
        return (label == lane_labels).astype(F32).astype(BF16)

    pole = (lat == n_lat - 1).astype(jnp.int32)
    row_eye = eye(rows)
    next_eye = eye(128)[:8]

    def mark_half(here, after, marks):
        def mark_column(col, _):
            for lev in range(LEV):
                labels = here[col, lev : lev + 1] * 2
                marks[lev, col, pl.ds(0, rows // 8)] = (
                    dot_nt(row_eye, one_hot(labels)).astype(BF16).reshape(rows // 8, 8, 128)
                )
                labels = after[col, lev : lev + 1] * 2 + pole
                marks[lev, col, rows // 8] = dot_nt(next_eye, one_hot(labels)).astype(BF16)
            return 0

        lax.fori_loop(0, 6, mark_column, 0)

    loads[1].wait()
    ahead[1].wait_recv()
    mark_half(own_region, own_next, own_marks)
    loads[3].wait()
    w_vt[...] = dot_nt(eye(channels), w_v[...]).astype(BF16)
    ahead[0].wait_recv()
    ahead[2].wait_recv()
    mark_half(east_region, east_next, east_marks)
    for load in (loads[0], loads[2], loads[4], loads[5]):
        load.wait()

    score_scale = 32 ** (-0.5) * 1.4426950408889634
    head_of_lane = lax.broadcasted_iota(jnp.int32, (SPAN, 128), 1) // 32
    head_of_row = lax.broadcasted_iota(jnp.int32, (128, 128), 0) // 32
    tail_head = lax.broadcasted_iota(jnp.int32, (128, 64), 1) // 16
    tail_row = lax.broadcasted_iota(jnp.int32, (128, 64), 0) // 32
    sum_row = lax.broadcasted_iota(jnp.int32, (16, 512), 0)
    sum_lane = lax.broadcasted_iota(jnp.int32, (16, 512), 1) // 128
    tail_sum_row = lax.broadcasted_iota(jnp.int32, (16, 64), 0)
    tail_sum_lane = lax.broadcasted_iota(jnp.int32, (16, 64), 1) // 16
    sum_rows = jnp.concatenate(
        [(sum_row == sum_lane).astype(F32), (tail_sum_row == tail_sum_lane).astype(F32)], 1
    ).astype(BF16)
    def stacked(value):
        return jnp.concatenate([value[:128]] * 4 + [value[128:]] * 4, 0)

    def window_parts(i):
        normed = ns[pl.ds(i * SPAN, SPAN)]
        value_t = dot_nt(
            w_vt[...], jnp.concatenate([normed[:128]] + [normed[128:]] * 4, 0)
        ).astype(BF16)
        marks = ms[pl.ds(i * SPAN, SPAN)]
        key_marks = stacked(((marks.astype(F32) - 1.0) * 1e30).astype(BF16))
        return value_t, marks, key_marks

    def scores_of(i, g, parts):
        base = i * SPAN
        lanes = pl.ds(g * 128, 128)
        query = jnp.concatenate([qs[pl.ds(base, SPAN), lanes], parts[1]], 1)
        key = ks[pl.ds(base, SPAN), lanes]
        heads = [jnp.where(head_of_lane == h, key, jnp.zeros_like(key)) for h in range(4)]
        keys = jnp.concatenate([k[:128] for k in heads] + [k[128:] for k in heads], 0)
        return dot_nt(jnp.concatenate([keys, parts[2]], 1), query)

    def weights_of(scores):
        mains, tails = [], []
        for h in range(4):
            main = scores[128 * h : 128 * h + 128]
            tail = scores[512 + 16 * h : 528 + 16 * h]
            peak = jnp.maximum(jnp.max(main, 0, keepdims=True), jnp.max(tail, 0, keepdims=True))
            mains.append(jnp.exp2((main - peak).astype(BF16)))
            tails.append(jnp.exp2((tail - peak).astype(BF16)))
        return jnp.concatenate(mains + tails, 0)

    def outs_of(g, parts, weights):
        group_values = parts[0][g * 128 : g * 128 + 128]
        main_values = group_values[:, :128]
        tail_values = group_values[:, 128:192]
        blocks = [
            jnp.where(head_of_row == h, main_values, jnp.zeros_like(main_values)) for h in range(4)
        ]
        blocks.append(jnp.where(tail_head == tail_row, tail_values, jnp.zeros_like(tail_values)))
        values = jnp.concatenate([jnp.concatenate(blocks, 1), sum_rows], 0)
        result = dot(values, weights)
        scale = 1.0 / result[128:136]
        return [result[32 * h : 32 * h + 32] * scale[h : h + 1] for h in range(4)]

    def attend_chunk():
        groups = HEADS // 4
        count = GROUP * groups
        parts, scores, weights, outs = {}, {}, {}, {i: [] for i in range(GROUP)}
        for t in range(count + 2):
            if t < count:
                i, g = divmod(t, groups)
                if g == 0:
                    parts[i] = window_parts(i)
                scores[t] = scores_of(i, g, parts[i])
            if 0 <= t - 2 < count:
                i, g = divmod(t - 2, groups)
                outs[i] += outs_of(g, parts[i], weights.pop(t - 2))
                if g == groups - 1:
                    out_t = jnp.concatenate(outs.pop(i), 0).astype(BF16)
                    wos[pl.ds(i * PADDED, PADDED)] = dot_nt(order[...], out_t).astype(BF16)
            if 0 <= t - 1 < count:
                weights[t - 1] = weights_of(scores.pop(t - 1))

    def merge(blocks):
        total = sum(jnp.sum(b, -1, keepdims=True) for b in blocks)
        mean = total * (1.0 / 2048)
        blocks = [b - mean for b in blocks]
        spread = sum(jnp.sum(b * b, -1, keepdims=True) for b in blocks) * (1.0 / 2048)
        factor = lax.rsqrt(spread + 1e-05)
        merge_in = jnp.concatenate([(b * factor).astype(BF16) for b in blocks], 1)
        return dot(merge_in, w_merge[...])

    def packed(rows40):
        stacked_lanes = jnp.concatenate([rows40[:, 512 * j : 512 * j + 512] for j in range(2)], 0)
        return dot(pack[...], stacked_lanes.astype(BF16)).astype(BF16)

    def own_copy():
        return pltpu.make_async_copy(
            stage.at[pl.ds(3 * lon, 3)], recv.at[lon], out_recv
        )

    def send_copy(owner):
        return pltpu.make_async_remote_copy(
            src_ref=stage.at[pl.ds(3 * owner, 3)],
            dst_ref=recv.at[lon],
            send_sem=out_send.at[owner],
            recv_sem=out_recv,
            device_id=(lat, owner),
            device_id_type=MESH,
        )

    def own_part(place, target, count):
        return pltpu.make_async_copy(
            stage.at[pl.ds(place, count)], recv.at[lon, pl.ds(target, count)], out_recv
        )

    def send_part(owner, place, target, count, sem):
        return remote(
            stage.at[pl.ds(place, count)],
            recv.at[lon, pl.ds(target, count)],
            out_send.at[sem],
            out_recv,
            (lat, owner),
        )

    def part_of(owner, place, target, count, sem):
        @pl.when(owner == lon)
        def _():
            own_part(place, target, count).start()

        @pl.when(owner != lon)
        def _():
            send_part(owner, place, target, count, sem).start()

    def last_copy():
        return pltpu.make_async_remote_copy(
            src_ref=stage.at[pl.ds(3 * windows, 1)],
            dst_ref=recv.at[lon, pl.ds(0, 1)],
            send_sem=out_send.at[windows],
            recv_sem=out_recv,
            device_id=(next_lat, 0),
            device_id_type=MESH,
        )

    def send(owner):
        @pl.when(owner == lon)
        def _():
            own_copy().start()

        @pl.when(owner != lon)
        def _():
            send_copy(owner).start()

    carry_copy = pltpu.make_async_remote_copy(
        src_ref=carry_send,
        dst_ref=carry_recv,
        send_sem=carry_sems.at[0],
        recv_sem=carry_sems.at[1],
        device_id=(next_lat, lon),
        device_id_type=MESH,
    )

    def finish_first(before, saved, place):
        pieces = [before[16 * p : 16 * p + 16] for p in range(2)]
        pieces += [odd_save[saved, pl.ds(16 * p, 16)] for p in range(2)]
        merged = jnp.concatenate([merge(pieces), jnp.zeros((24, 2 * channels), F32)], 0)
        stage[place] = packed(merged)[:24].reshape(3, 8, 512)

    carry[...] = jnp.zeros_like(carry)
    slot_row = lax.broadcasted_iota(jnp.int32, (GROUP * 40, 512), 0) % 40 < 12

    def chunk_step(step, _):
        chunk = lax.rem(first + step, chunks)
        start = chunk * GROUP

        halo_case(chunk, first, lambda copy: copy.wait_recv())

        @pl.when(chunk == chunks - 1)
        def _():
            for half, target in enumerate((own, east)):
                ahead[3 + half].wait_recv()
                top = dot(spread_top, top_recv[half].reshape(40, channels)).astype(BF16)
                target[:, :, rows // 8] = top.reshape(LEV, 6, 8, channels)

        for i in range(GROUP):
            part = pl.ds(3 * chunk + PICK_STARTS[i], 2)
            raw = [
                jnp.concatenate(
                    [value[:, :, part].reshape(BLOCK, channels), marks[:, :, part].reshape(BLOCK, 128)],
                    1,
                )
                for value, marks in ((own, own_marks), (east, east_marks))
            ]
            value = dot(pick[i], jnp.concatenate(raw, 0))
            ms[pl.ds(i * SPAN, SPAN)] = value[:, channels:].astype(BF16)
            value = value[:, :channels]
            xs[pl.ds(i * SPAN, SPAN)] = value.astype(BF16)
            ns[pl.ds(i * SPAN, SPAN)] = normalize(value).astype(BF16)
        qs[...] = (dot(ns[...], w_qk[:, :512]) * score_scale).astype(BF16)
        ks[...] = dot(ns[...], w_qk[:, 512:]).astype(BF16)
        attend_chunk()
        residual = jnp.concatenate(
            [dot(order[...], xs[pl.ds(i * SPAN, SPAN)]) for i in range(GROUP)], 0
        )
        updated = (residual + dot(wos[...], w_out[...])).astype(BF16).astype(F32)
        blocks = []
        for p in range(4):
            pieces = [
                updated[PADDED * i + 40 * p : PADDED * i + 40 * p + 40] for i in range(GROUP)
            ]
            block = jnp.concatenate(pieces, 0)
            if p < 2:
                before = jnp.concatenate([carry[pl.ds(40 * p, 40)]] + pieces[:-1], 0)
                carry[pl.ds(40 * p, 40)] = pieces[-1]
                block = jnp.where(slot_row, before, block)
            blocks.append(block)

        @pl.when(step == 0)
        def _():
            for p in range(2):
                odd_save[1, pl.ds(16 * p, 16)] = blocks[2 + p][:16]

        @pl.when(chunk == 0)
        def _():
            for p in range(2):
                odd_save[0, pl.ds(16 * p, 16)] = blocks[2 + p][:16]

        @pl.when(chunk == chunks - 1)
        def _():
            for p in range(2):
                carry_send[pl.ds(16 * p, 16)] = carry[pl.ds(40 * p, 16)].astype(BF16)
            carry_copy.start()

        merged = merge(blocks)
        for i in range(GROUP):
            pieces = packed(merged[40 * i : 40 * i + 40])
            for slot in range(3):
                stage[3 * (start + i) + 1 + slot] = pieces[24 * slot : 24 * slot + 24].reshape(3, 8, 512)
            owner = start + i
            if i == 0:

                @pl.when(jnp.logical_and(step > 0, chunk > 0))
                def _():
                    send(owner)

                @pl.when(chunk == 0)
                def _():
                    part_of(0, 2, 2, 1, 0)

                @pl.when(jnp.logical_and(step == 0, chunk > 0))
                def _():
                    part_of(owner, 3 * owner + 2, 2, 1, owner)
            else:
                send(owner)

        @pl.when(chunk == chunks - 1)
        def _():
            last_copy().start()

        @pl.when(jnp.logical_and(step == chunks - 1, first != 0))
        def _():
            carry_copy.wait_recv()
            finish_first(carry_recv[...].astype(F32), 0, 1)
            part_of(0, 1, 1, 1, windows + 1)

        return 0

    lax.fori_loop(0, chunks, chunk_step, 0)

    @pl.when(first == 0)
    def _():
        carry_copy.wait_recv()
        finish_first(carry_recv[...].astype(F32), 0, 1)
        part_of(0, 1, 1, 1, windows + 1)

    split = GROUP * first

    @pl.when(first != 0)
    def _():
        last = jnp.concatenate([carry[pl.ds(40 * p, 16)] for p in range(2)], 0)
        finish_first(last, 1, 3 * split + 1)
        part_of(split, 3 * split, 0, 2, windows + 2)

    def wait_halo(chunk, _):
        halo_case(chunk, first_west, lambda copy: copy.wait_send())
        return 0

    lax.fori_loop(0, chunks, wait_halo, 0)
    for copy in ahead:
        copy.wait_send()
    carry_copy.wait_send()
    last_copy().wait_send()

    @pl.when(lon != 0)
    def _():
        send_part(0, 2, 2, 1, 0).wait_send()
        send_part(0, 1, 1, 1, windows + 1).wait_send()

    @pl.when(jnp.logical_and(first != 0, split != lon))
    def _():
        send_part(split, 3 * split + 2, 2, 1, split).wait_send()
        send_part(split, 3 * split, 0, 2, windows + 2).wait_send()

    def wait_send(owner, _):
        @pl.when(jnp.logical_and(owner != lon, owner != split))
        def _():
            send_copy(owner).wait_send()

        return 0

    lax.fori_loop(1, windows, wait_send, 0)
    pltpu.make_async_copy(recv, recv, out_recv).wait()


def exchange(tokens, region, w_qkv, w_out, w_merge, n_lat, n_lon):
    levels, cols, tiles, _, channels = tokens.shape
    rows = tiles * 8
    windows = rows // WIN_LAT
    vmem = pl.BlockSpec(memory_space=pltpu.VMEM)
    hbm = pl.BlockSpec(memory_space=pl.ANY)
    span = GROUP * SPAN
    half = cols // 2
    return pl.pallas_call(
        functools.partial(fused, n_lat, n_lon),
        out_shape=jax.ShapeDtypeStruct((n_lon, 3, 3, 8, 512), BF16),
        in_specs=[hbm] * 2 + [vmem] * 3 + [hbm] * 3,
        out_specs=hbm,
        scratch_shapes=[
            pltpu.VMEM((levels, half, tiles + 1, 8, channels), BF16),
            pltpu.VMEM((levels, half, tiles + 1, 8, channels), BF16),
            pltpu.VMEM((half, levels, rows), jnp.int32),
            pltpu.VMEM((half, levels, rows), jnp.int32),
            pltpu.VMEM((half, levels, 128), jnp.int32),
            pltpu.VMEM((half, levels, 128), jnp.int32),
            pltpu.VMEM((levels, half, tiles + 1, 8, 128), BF16),
            pltpu.VMEM((levels, half, tiles + 1, 8, 128), BF16),
            pltpu.VMEM((3 * windows + 1, 3, 8, 512), BF16),
            pltpu.VMEM((channels, 2 * channels), BF16),
            pltpu.VMEM((channels, channels), BF16),
            pltpu.VMEM((channels, channels), BF16),
            pltpu.VMEM((channels, channels), BF16),
            pltpu.VMEM((4 * channels, 2 * channels), BF16),
            pltpu.VMEM((span, channels), BF16),
            pltpu.VMEM((span, channels), BF16),
            pltpu.VMEM((span, 128), BF16),
            pltpu.VMEM((span, channels), BF16),
            pltpu.VMEM((span, channels), BF16),
            pltpu.VMEM((GROUP * PADDED, channels), BF16),
            pltpu.VMEM((80, channels), F32),
            pltpu.VMEM((2, 32, channels), F32),
            pltpu.VMEM((32, channels), BF16),
            pltpu.VMEM((32, channels), BF16),
            pltpu.VMEM((levels, cols, 1, 8, channels), BF16),
            pltpu.VMEM((2, 5, 8, channels), BF16),
            pltpu.VMEM((2, 5, 8, channels), BF16),
            pltpu.SemaphoreType.DMA((7,)),
            pltpu.SemaphoreType.DMA((5,)),
            pltpu.SemaphoreType.DMA((5,)),
            pltpu.SemaphoreType.DMA((windows // GROUP,)),
            pltpu.SemaphoreType.DMA((windows // GROUP,)),
            pltpu.SemaphoreType.DMA((2,)),
            pltpu.SemaphoreType.DMA((windows + 3,)),
            pltpu.SemaphoreType.DMA,
        ],
        compiler_params=pltpu.CompilerParams(
            collective_id=0, has_side_effects=True, vmem_limit_bytes=56 * 1024 * 1024
        ),
        name="attend_merge_send",
    )(tokens, region, *tables(), w_qkv, w_out, w_merge)


def place(table, pieces, out):
    sources = pieces.shape[0]
    for group in range(sources // 8):
        before = pieces[(8 * group + sources - 1) % sources, 0].reshape(24, 512)
        here = pieces[8 * group : 8 * group + 8, 0].reshape(192, 512)
        columns = dot(table[...], jnp.concatenate([before, here], 0)).astype(BF16)
        for lanes in range(2):
            out[0, 0, 48 * group : 48 * group + 48, 512 * lanes : 512 * lanes + 512] = columns[
                48 * lanes : 48 * lanes + 48
            ]


def arrange(recv):
    n_lon = recv.shape[0]
    return pl.pallas_call(
        place,
        grid=(3, LEV),
        out_shape=jax.ShapeDtypeStruct((LEV, 3, n_lon * 6, 1024), BF16),
        in_specs=[
            pl.BlockSpec((96, 216), lambda row, lev: (lev, 0)),
            pl.BlockSpec((n_lon, 1, 3, 8, 512), lambda row, lev: (0, row, 0, 0, 0)),
        ],
        out_specs=pl.BlockSpec((1, 1, n_lon * 6, 1024), lambda row, lev: (lev, row, 0, 0)),
        name="place_columns",
    )(arrange_table(), recv)


def solution(mesh):
    n_lat, n_lon = mesh.shape["lat"], mesh.shape["lon"]

    def body(tokens, region, w_qkv, w_out, w_merge):
        levels, rows, cols, channels = tokens.shape
        by_column = tokens.transpose(0, 2, 1, 3).reshape(levels, cols, rows // 8, 8, channels)
        recv = exchange(
            by_column, region.transpose(2, 0, 1), w_qkv, w_out, w_merge, n_lat, n_lon
        )
        return arrange(recv)

    in_specs = (P(None, "lat", "lon", None), P(None, "lat", "lon"), P(), P(), P())
    out_specs = P(None, ("lat", "lon"), None, None)
    return jax.shard_map(body, mesh=mesh, in_specs=in_specs, out_specs=out_specs, check_vma=False)
```
